512 devices in a mesh: row: 8 (over y_lo, x), col: 8 (over y_hi, core), depth: 8 (over z).
Axes of the slice: x: 4, y: 8 (y_hi: 4, y_lo: 2; y = y_hi * 2 + y_lo), z: 8, core: 2. Of those that a mesh axis runs over, the one named last changes fastest.
Arguments:
- residual: bfloat16 [1024, 4096], P(('row', 'depth'), 'col'), may hold values from -48 to 48
- pre_gain: float32 [4096], P('col'), may hold values from 0.1 to 1.9
- w_gate: bfloat16 [4096, 16384], P('row', ('col', 'depth')), may hold values from -0.09375 to 0.09375
- w_up: bfloat16 [4096, 16384], P('row', ('col', 'depth')), may hold values from -0.09375 to 0.09375
- w_down: bfloat16 [16384, 4096], P(('col', 'depth'), 'row'), may hold values from -0.125 to 0.125
- value_head: float32 [4096], P('col'), may hold values from -0.0234375 to 0.0234375
- sample_index: int32 [1024], P(('row', 'depth')), may hold values from 0 to 32767
- return_table: float32 [32768], replicated, may hold values from -6 to 6
Outputs:
- values: float32 [1024], P(('row', 'depth'))
- grad_gate_weight: bfloat16 [4096, 16384], P('row', ('col', 'depth'))
- grad_up_weight: bfloat16 [4096, 16384], P('row', ('col', 'depth'))
- grad_down_weight: bfloat16 [16384, 4096], P(('col', 'depth'), 'row')
- grad_value: float32 [4096], P('col')
The draws below stay inside these ranges and needn't reach their ends.
All inputs are finite; a program needn't handle non-finite values.
Results may differ from the reference program's by a relative error of at most 0.013.
Values may be sent and summed in bfloat16 or wider, within the bound.
A program may use at most 64 MiB of HBM per device.

```python
import jax
import jax.numpy as jnp
from jax import lax

D = 4096
FF = 16384
BUF = 32768
TOKENS = 1024


def shared_signs(key):
    return (2 * jax.random.randint(key, (D,), 0, 2) - 1).astype(jnp.float32)


def draw_residual(key, part):
    signs = shared_signs(key)
    key = jax.random.fold_in(key, 11)
    key_entries, key_columns, key_rows, key_tilt = jax.random.split(key, 4)
    position = jnp.arange(D, dtype=jnp.float32) / D
    rising = 0.6 * jnp.exp(jnp.log(3.0) * (position - 0.5))
    column_scale = rising * jnp.exp(jax.random.uniform(key_columns, (D,), jnp.float32, -1.1513, 1.1513))
    row_scale = jnp.exp(jax.random.uniform(key_rows, (TOKENS, 1), jnp.float32, -1.1513, 1.1513))
    tilt = jax.random.uniform(key_tilt, (TOKENS, 1), jnp.float32, -1.5, 1.5)
    entries = jax.random.truncated_normal(key_entries, -3.0, 3.0, (TOKENS, D), jnp.float32)
    mixed = entries + tilt * signs[None, :]
    return (mixed * row_scale * column_scale[None, :]).astype(jnp.bfloat16)


def draw_value_head(key, part):
    signs = shared_signs(key)
    key = jax.random.fold_in(key, 23)
    magnitude = jax.random.uniform(key, (D,), jnp.float32, 0.5, 1.49)
    return (signs * magnitude / jnp.sqrt(jnp.float32(D))).astype(jnp.float32)


def plant(values, rng, smallest, high):
    longest = values.shape.index(max(values.shape))
    spots = []
    for shift in (0, 1):
        where = [jax.random.randint(jax.random.fold_in(rng, axis), (), 0, length) for axis, length in enumerate(values.shape)]
        where[longest] = (where[longest] + shift) % values.shape[longest]
        spots.append(tuple(where))
    return values.at[spots[0]].set(smallest).at[spots[1]].set(high)


def strengthened(values, rng, source, target, blocks, factor):
    def block_of(dim):
        return (jnp.arange(values.shape[dim]) // (values.shape[dim] // blocks)).reshape((-1,) + (1,) * (values.ndim - 1 - dim))

    one_side = jax.random.permutation(rng, blocks)[block_of(target)]
    second = (block_of(target) + blocks // 2) % blocks
    return jnp.where((block_of(source) == one_side) | (block_of(source) == second), factor * values, values)


def level_of(key, extent, pieces, least, largest):
    level = 1.0
    for axis_at, shards_of in pieces:
        heights = jax.random.uniform(jax.random.fold_in(jax.random.fold_in(key, 6), axis_at), (shards_of,), jnp.float32, least / len(pieces), largest / len(pieces))
        level = level * jnp.repeat(jnp.exp(heights), extent[axis_at] // shards_of).reshape((-1,) + (1,) * (len(extent) - 1 - axis_at))
    return level


def gaussian(key, shape, spread, limit, pieces=(), kind=jnp.bfloat16):
    values = jax.random.normal(key, shape, jnp.float32) * spread
    if len(pieces) > 0:
        values = level_of(key, shape, pieces, -0.22, 0.18) * values
    return jnp.clip(values, min=-limit, max=limit).astype(kind)


def heavy_noise(rng, shape, spread, most, cuts, heavy, held_as=jnp.bfloat16):
    drawn = spread * jax.random.normal(rng, shape, jnp.float32)
    if cuts:
        drawn = drawn * level_of(rng, shape, cuts, -0.22, 0.18)
    return jnp.clip(strengthened(drawn, jax.random.fold_in(rng, 3), *heavy), -most, most).astype(held_as)


def setup_inputs(seed: int = 0) -> dict:
    streams_of = jax.random.split(jax.random.key(seed), 9)
    return {
        "residual": draw_residual(jax.random.fold_in(streams_of[8], 71), 0),
        "pre_gain": jnp.clip(1.0 + 0.18 * jax.random.normal(streams_of[1], (D,), jnp.float32), 0.1, 1.9),
        "w_gate": gaussian(streams_of[2], (D, FF), D ** -0.5, 0.09375, ((0, 8), (1, 64))),
        "w_up": gaussian(streams_of[3], (D, FF), D ** -0.5, 0.09375, ((0, 8), (1, 64))),
        "w_down": heavy_noise(streams_of[4], (FF, D), FF ** -0.5, 0.125, ((0, 64), (1, 8)), (0, 1, 64, 4.0)),
        "value_head": draw_value_head(jax.random.fold_in(streams_of[8], 71), 0),
        "sample_index": plant(jax.random.randint(streams_of[6], (TOKENS,), 0, BUF), jax.random.fold_in(streams_of[6], 1), 0, BUF - 1).astype(jnp.int32),
        "return_table": gaussian(streams_of[7], (BUF,), 1.5, 6.0, (), jnp.float32),
    }


norm_eps = 1e-06
huber_delta = 1.0

def contract_rows(left, right):
    return lax.dot_general(left, right, (((0,), (0,)), ((), ())), preferred_element_type=jnp.float32)

def reference(residual, pre_gain, w_gate, w_up, w_down, value_head, sample_index, return_table):
    wide = residual.astype(jnp.float32)
    inv_norm = lax.rsqrt(lax.optimization_barrier(jnp.mean(wide * wide, axis=1, keepdims=True)) + norm_eps)
    normed = (wide * inv_norm * pre_gain[None, :]).astype(jnp.bfloat16)
    gate_value = jnp.dot(normed, w_gate, preferred_element_type=jnp.float32)
    up_value = jnp.dot(normed, w_up, preferred_element_type=jnp.float32)
    sigmoid_gate = jax.nn.sigmoid(gate_value)
    hidden = (gate_value * sigmoid_gate * up_value).astype(jnp.bfloat16)
    output = wide + jnp.dot(hidden, w_down, preferred_element_type=jnp.float32)
    inv_final = lax.rsqrt(lax.optimization_barrier(jnp.mean(output * output, axis=1, keepdims=True)) + norm_eps)
    final = output * inv_final
    values = lax.optimization_barrier(jnp.sum(final * value_head[None, :], axis=1))
    target = jnp.take(return_table, sample_index.astype(jnp.int32))
    slope = jnp.clip(values - target, -huber_delta, huber_delta)
    grad_value = lax.optimization_barrier(jnp.sum(final * slope[:, None], axis=0))
    grad_final = slope[:, None] * value_head[None, :]
    inner = lax.optimization_barrier(jnp.mean(grad_final * final, axis=1, keepdims=True))
    grad_output = (inv_final * (grad_final - final * inner)).astype(jnp.bfloat16)
    grad_hidden = lax.dot_general(grad_output, w_down, (((1,), (1,)), ((), ())), preferred_element_type=jnp.float32)
    grad_gate = (grad_hidden * up_value * sigmoid_gate * (1.0 + gate_value * (1.0 - sigmoid_gate))).astype(jnp.bfloat16)
    grad_up = (grad_hidden * gate_value * sigmoid_gate).astype(jnp.bfloat16)
    grad_down_weight = contract_rows(hidden, grad_output).astype(jnp.bfloat16)
    grad_gate_weight = contract_rows(normed, grad_gate).astype(jnp.bfloat16)
    grad_up_weight = contract_rows(normed, grad_up).astype(jnp.bfloat16)
    return (values, grad_gate_weight, grad_up_weight, grad_down_weight, grad_value)
```

```python
import functools

import jax
import jax.numpy as jnp
from jax import lax
from jax.experimental import pallas as pl
from jax.experimental.pallas import tpu as pltpu
from jax.sharding import PartitionSpec as P

MESH = pl.DeviceIdType.MESH
norm_eps = 1e-06
huber_delta = 1.0


def rem(value, size):
    return lax.rem(value, jnp.int32(size))


def dot(left, right):
    return jnp.dot(left, right, preferred_element_type=jnp.float32)


def kernel(
    R, YH, Z, B, F, H,
    x_ref, gv_ref, tgt_ref, wg_ref, wu_ref, wd_ref,
    dg_ref, du_ref, dd_ref, val_ref, gval_ref,
    xbuf, ybuf, ytbuf, rssend, rsrecv, guown, st1send, st1recv,
    hbuf, htbuf, gatebuf, upbuf, invbuf,
    osend, osib, oown, zsend, zrecv, ysend, yrecv, obuf,
    st2send, st2recv, abuf, bbuf, gobuf, ghsend, ghrecv, ghown, ggbuf,
    gvbuf, gvsend, gvrecv, tg1, tg2send, tg2,
    s1_s, s1_r, gv_s, gv_r, t1_s, t1_r, t2_s, t2_r,
    z1_s, z1_r, b1_s, b1_r, rs_s, rs_r, q1_s, q1_r, h_s, h_r,
    ob_s, ob_r, oz_s, oz_r, oy_s, oy_r, ay_s, ay_r, az_s, az_r, ab_s, ab_r,
    q2_s, q2_r, gh_s, gh_r, gg_s, gg_r, go_s, go_r,
):
    r = lax.axis_index("row")
    c = lax.axis_index("col")
    d = lax.axis_index("depth")
    core = rem(c, 2)
    yh = lax.div(c, jnp.int32(2))
    rpar = rem(r, 2)
    rj = lax.div(r, jnp.int32(2))
    T = 2 * YH * B
    half = YH * B
    features = R * F
    diagonal = r == c

    def copy(src, dst, send, recv, device):
        return pltpu.make_async_remote_copy(
            src_ref=src, dst_ref=dst, send_sem=send, recv_sem=recv,
            device_id=device, device_id_type=MESH,
        )

    def row_peer(k):
        return rem(r + k, R)

    def depth_peer(k):
        return rem(d + k, Z)

    def y_peer(k):
        return rem(yh + k, YH)

    def row_device(q):
        return (q, c, d)

    def depth_device(q):
        return (r, c, q)

    def y_device(j):
        return (r, 2 * j + core, d)

    sibling = (r, 2 * yh + 1 - core, d)
    partner = (c, r, d)
    mine = pl.ds(pl.multiple_of(core * half, 16), half)
    other = pl.ds(pl.multiple_of((1 - core) * half, 16), half)

    def slot(parity, j):
        return pl.ds(pl.multiple_of(parity * half + j * B, 16), B)

    def loop(count, body, start=0):
        def step(k, carry):
            body(k)
            return carry
        lax.fori_loop(start, count, step, 0)

    eye = (
        lax.broadcasted_iota(jnp.int32, (T, T), 0)
        == lax.broadcasted_iota(jnp.int32, (T, T), 1)
    )

    def to_lanes(column):
        return jnp.sum(jnp.where(eye, column, 0.0), axis=0, keepdims=True)

    def to_column(lanes):
        return jnp.sum(jnp.where(eye, lanes, 0.0), axis=1, keepdims=True)

    barrier = pltpu.get_barrier_semaphore()

    def greet(device):
        pl.semaphore_signal(barrier, inc=1, device_id=device, device_id_type=MESH)

    for k in range(1, R):
        greet(row_device(row_peer(k)))
    for k in range(1, Z):
        greet(depth_device(depth_peer(k)))
    for k in range(1, YH):
        greet(y_device(y_peer(k)))
    greet(sibling)
    for j in range(YH):
        @pl.when(jnp.logical_not(diagonal & (yh == j)))
        def _():
            greet((2 * j + core, r, d))
    pl.semaphore_wait(
        barrier, (R - 1) + (Z - 1) + (YH - 1) + 1 + YH - jnp.where(diagonal, 1, 0)
    )

    def first_copy(j):
        return copy(
            x_ref, xbuf.at[d, slot(rpar, rj)], s1_s.at[j], s1_r.at[rj],
            (c, 2 * j + rpar, d),
        )

    def first_arrival(j):
        return copy(
            x_ref, xbuf.at[d, slot(core, j)], s1_s.at[j], s1_r.at[j],
            (2 * j + core, r, d),
        )

    for j in range(YH):
        local = diagonal & (yh == j)

        @pl.when(local)
        def _():
            xbuf[d, slot(core, j)] = x_ref[...]

        @pl.when(jnp.logical_not(local))
        def _():
            first_copy(j).start()

    gv_copy = copy(gv_ref, gvbuf, gv_s, gv_r, partner)

    @pl.when(diagonal)
    def _():
        gvbuf[...] = gv_ref[...]

    @pl.when(jnp.logical_not(diagonal))
    def _():
        gv_copy.start()

    def t1_copy(k):
        return copy(tgt_ref, tg1.at[r], t1_s.at[k], t1_r.at[k], row_device(row_peer(k)))

    def t1_arrival(k):
        q = row_peer(R - k)
        return copy(tgt_ref, tg1.at[q], t1_s.at[k], t1_r.at[k], row_device(q))

    for k in range(1, R):
        t1_copy(k).start()

    for j in range(YH):
        @pl.when(jnp.logical_not(diagonal & (yh == j)))
        def _():
            first_arrival(j).wait_recv()

    def gather_over_depth(buf, zs, zr, bs, br):
        def z_copy(k):
            return copy(
                buf.at[d, mine], buf.at[d, mine], zs.at[k], zr.at[k],
                depth_device(depth_peer(k)),
            )

        def z_arrival(k):
            q = depth_peer(Z - k)
            return copy(
                buf.at[q, mine], buf.at[q, mine], zs.at[k], zr.at[k], depth_device(q)
            )

        def s_copy(k):
            q = depth_peer(Z - k)
            return copy(buf.at[q, mine], buf.at[q, mine], bs.at[k], br.at[k], sibling)

        def s_arrival(k):
            q = depth_peer(Z - k)
            return copy(buf.at[q, other], buf.at[q, other], bs.at[k], br.at[k], sibling)

        return z_copy, z_arrival, s_copy, s_arrival

    near = []
    for k in range(1, Z // 2 + 1):
        near.append(k)
        if Z - k > k:
            near.append(Z - k)

    z_copy, z_arrival, s_copy, s_arrival = gather_over_depth(xbuf, z1_s, z1_r, b1_s, b1_r)
    for k in near:
        z_copy(k).start()
    s_copy(0).start()

    total = tgt_ref[...]
    for k in range(1, R):
        t1_arrival(k).wait_recv()
        total = total + tg1[row_peer(R - k)]
    tg2send[...] = total

    def t2_copy(k):
        return copy(tg2send, tg2.at[d], t2_s.at[k], t2_r.at[k], depth_device(depth_peer(k)))

    def t2_arrival(k):
        q = depth_peer(Z - k)
        return copy(tg2send, tg2.at[q], t2_s.at[k], t2_r.at[k], depth_device(q))

    for k in range(1, Z):
        t2_copy(k).start()

    for k in near:
        z_arrival(k).wait_recv()
        s_copy(k).start()

    @pl.when(jnp.logical_not(diagonal))
    def _():
        gv_copy.wait_recv()

    for k in range(Z):
        s_arrival(k).wait_recv()

    gain = gvbuf[0:1, :]

    def rs_copy(q):
        return copy(rssend.at[q], rsrecv.at[r], rs_s.at[q], rs_r.at[r], row_device(q))

    def rs_arrival(q):
        return copy(rssend.at[q], rsrecv.at[q], rs_s.at[q], rs_r.at[q], row_device(q))

    def q1_copy(q):
        return copy(st1send.at[q], st1recv.at[r], q1_s.at[q], q1_r.at[r], row_device(q))

    def q1_arrival(q):
        return copy(st1send.at[q], st1recv.at[q], q1_s.at[q], q1_r.at[q], row_device(q))

    def gate_up(q):
        wide = xbuf[q].astype(jnp.float32)
        squares = jnp.sum(wide * wide, axis=1, keepdims=True)
        st1send[q] = jnp.broadcast_to(to_lanes(squares), (8, T))
        scaled = (wide * gain).astype(jnp.bfloat16)
        ybuf[q] = scaled
        return dot(scaled, wg_ref[...]), dot(scaled, wu_ref[...])

    def gate_up_step(k):
        q = row_peer(k)
        gate, up = gate_up(q)
        q1_copy(q).start()
        rssend[q, :, 0:H] = gate.astype(jnp.bfloat16)
        rssend[q, :, H:2 * H] = up.astype(jnp.bfloat16)
        rs_copy(q).start()

    loop(R, gate_up_step, 1)
    gate, up = gate_up(r)
    guown[:, 0:H] = gate
    guown[:, H:2 * H] = up

    def transpose_step(q):
        ytbuf[:, pl.ds(pl.multiple_of(q * T, T), T)] = ybuf[q].T

    loop(Z, transpose_step)

    squares = st1send[r]
    for k in range(1, R):
        q = row_peer(k)
        q1_arrival(q).wait_recv()
        squares = squares + st1recv[q]
    inv_norm = to_column(lax.rsqrt(squares / features + norm_eps)[0:1, :])
    invbuf[...] = inv_norm

    def gate_sum_step(k):
        q = row_peer(k)
        rs_arrival(q).wait_recv()
        guown[...] += rsrecv[q].astype(jnp.float32)

    loop(R, gate_sum_step, 1)
    gate = guown[:, 0:H] * invbuf[...]
    up = guown[:, H:2 * H] * invbuf[...]
    gatebuf[...] = gate
    upbuf[...] = up
    hbuf[r] = (gate * jax.nn.sigmoid(gate) * up).astype(jnp.bfloat16)

    def h_copy(q):
        return copy(hbuf.at[r], hbuf.at[r], h_s.at[q], h_r.at[r], row_device(q))

    def h_arrival(q):
        return copy(hbuf.at[q], hbuf.at[q], h_s.at[q], h_r.at[q], row_device(q))

    for k in range(1, R):
        h_copy(row_peer(k)).start()

    def ob_copy(q):
        return copy(osend.at[q, other], osib.at[q], ob_s.at[q], ob_r.at[q], sibling)

    def ob_arrival(q):
        return copy(osend.at[q, mine], osib.at[q], ob_s.at[q], ob_r.at[q], sibling)

    def oz_copy(q):
        return copy(zsend.at[q], zrecv.at[d], oz_s.at[q], oz_r.at[d], depth_device(q))

    def oz_arrival(q):
        return copy(zsend.at[q], zrecv.at[q], oz_s.at[q], oz_r.at[q], depth_device(q))

    def down_step(k):
        q = depth_peer(k)

        @pl.when(q != r)
        def _():
            h_arrival(q).wait_recv()

        osend[q] = dot(hbuf[q], wd_ref[...]).astype(jnp.bfloat16)
        ob_copy(q).start()

    loop(Z + 1, down_step, 1)

    def pair_step(k):
        q = depth_peer(k)
        ob_arrival(q).wait_recv()
        zsend[q] = (
            osend[q, mine].astype(jnp.float32) + osib[q].astype(jnp.float32)
        ).astype(jnp.bfloat16)
        oz_copy(q).start()

    loop(Z, pair_step, 1)
    ob_arrival(d).wait_recv()
    oown[...] = osend[d, mine].astype(jnp.float32) + osib[d].astype(jnp.float32)

    def transpose_hidden_step(q):
        htbuf[:, pl.ds(pl.multiple_of(q * T, T), T)] = hbuf[q].T

    loop(R, transpose_hidden_step)

    def depth_sum_step(k):
        q = depth_peer(k)
        oz_arrival(q).wait_recv()
        oown[...] += zrecv[q].astype(jnp.float32)

    loop(Z, depth_sum_step, 1)
    ysend[...] = oown[...].astype(jnp.bfloat16)

    def block(j):
        return pl.ds(pl.multiple_of(j * B, 16), B)

    def oy_copy(j):
        return copy(ysend.at[block(j)], yrecv.at[yh], oy_s.at[j], oy_r.at[yh], y_device(j))

    def oy_arrival(j):
        return copy(ysend.at[block(j)], yrecv.at[j], oy_s.at[j], oy_r.at[j], y_device(j))

    for k in range(1, YH):
        oy_copy(y_peer(k)).start()
    output = oown[block(yh)] + xbuf[d, slot(core, yh)].astype(jnp.float32)
    for k in range(1, YH):
        j = y_peer(k)
        oy_arrival(j).wait_recv()
        output = output + yrecv[j].astype(jnp.float32)
    obuf[d, slot(core, yh)] = output.astype(jnp.bfloat16)

    def ay_copy(j):
        part = obuf.at[d, slot(core, yh)]
        return copy(part, part, ay_s.at[j], ay_r.at[yh], y_device(j))

    def ay_arrival(j):
        part = obuf.at[d, slot(core, j)]
        return copy(part, part, ay_s.at[j], ay_r.at[j], y_device(j))

    for k in range(1, YH):
        ay_copy(y_peer(k)).start()
    for k in range(1, YH):
        ay_arrival(y_peer(k)).wait_recv()
    a_copy, a_arrival, as_copy, as_arrival = gather_over_depth(obuf, az_s, az_r, ab_s, ab_r)
    for k in near:
        a_copy(k).start()
    as_copy(0).start()
    for k in near:
        a_arrival(k).wait_recv()
        as_copy(k).start()

    head = gvbuf[1:2, :]

    def stat_step(k):
        q = depth_peer(Z - k)
        as_arrival(k).wait_recv()
        wide = obuf[q].astype(jnp.float32)
        st2send[pl.ds(q, 1), :] = to_lanes(jnp.sum(wide * wide, axis=1, keepdims=True))
        st2send[pl.ds(Z + q, 1), :] = to_lanes(jnp.sum(wide * head, axis=1, keepdims=True))

    loop(Z, stat_step)

    def q2_copy(q):
        return copy(st2send, st2recv.at[r], q2_s.at[q], q2_r.at[r], row_device(q))

    def q2_arrival(q):
        return copy(st2send, st2recv.at[q], q2_s.at[q], q2_r.at[q], row_device(q))

    for k in range(1, R):
        q2_copy(row_peer(k)).start()

    target = tg2send[...]
    for k in range(1, Z):
        t2_arrival(k).wait_recv()
        target = target + tg2[depth_peer(Z - k)]

    sums = st2send[...]
    for k in range(1, R):
        q = row_peer(k)
        q2_arrival(q).wait_recv()
        sums = sums + st2recv[q]
    inv_final = lax.rsqrt(sums[0:Z] / features + norm_eps)
    values = sums[Z:2 * Z] * inv_final
    val_ref[...] = values
    slope = jnp.clip(values - target[0:Z], -huber_delta, huber_delta)
    abuf[...] = inv_final * slope
    bbuf[...] = inv_final * inv_final * (slope * values / features)

    def gh_copy(q):
        return copy(ghsend.at[q], ghrecv.at[r], gh_s.at[q], gh_r.at[r], row_device(q))

    def gh_arrival(q):
        return copy(ghsend.at[q], ghrecv.at[q], gh_s.at[q], gh_r.at[q], row_device(q))

    gvsend[...] = jnp.zeros_like(gvsend)

    def grad_hidden(q):
        wide = obuf[q].astype(jnp.float32)
        scale = to_column(abuf[pl.ds(q, 1), :])
        shrink = to_column(bbuf[pl.ds(q, 1), :])
        grad = (scale * head - shrink * wide).astype(jnp.bfloat16)
        gobuf[q] = grad
        gvsend[...] += jnp.broadcast_to(
            jnp.sum(wide * scale, axis=0, keepdims=True), gvsend.shape
        )
        return lax.dot_general(
            grad, wd_ref[...], (((1,), (1,)), ((), ())), preferred_element_type=jnp.float32
        )

    def grad_hidden_step(k):
        q = row_peer(k)
        ghsend[q] = grad_hidden(q).astype(jnp.bfloat16)
        gh_copy(q).start()

    loop(R, grad_hidden_step, 1)
    ghown[...] = grad_hidden(r)

    go_copy = copy(gvsend, gvrecv, go_s, go_r, partner)

    @pl.when(diagonal)
    def _():
        gvrecv[...] = gvsend[...]

    @pl.when(jnp.logical_not(diagonal))
    def _():
        go_copy.start()

    def hidden_sum_step(k):
        q = row_peer(k)
        gh_arrival(q).wait_recv()
        ghown[...] += ghrecv[q].astype(jnp.float32)

    loop(R, hidden_sum_step, 1)
    gate = gatebuf[...]
    up = upbuf[...]
    sig = jax.nn.sigmoid(gate)
    grad = ghown[...] * invbuf[...]
    ggbuf[r, :, 0:H] = (grad * up * sig * (1.0 + gate * (1.0 - sig))).astype(jnp.bfloat16)
    ggbuf[r, :, H:2 * H] = (grad * gate * sig).astype(jnp.bfloat16)

    def gg_copy(q):
        return copy(ggbuf.at[r], ggbuf.at[r], gg_s.at[q], gg_r.at[r], row_device(q))

    def gg_arrival(q):
        return copy(ggbuf.at[q], ggbuf.at[q], gg_s.at[q], gg_r.at[q], row_device(q))

    for k in range(1, R):
        gg_copy(row_peer(k)).start()

    tokens = Z * T
    tile = min(128, H)

    def down_weight_step(m):
        rows = pl.ds(pl.multiple_of(m * tile, tile), tile)
        dd_ref[rows, :] = dot(
            htbuf[rows, :], gobuf[...].reshape(tokens, F)
        ).astype(jnp.bfloat16)

    loop(H // tile, down_weight_step)

    for k in range(1, R):
        gg_arrival(row_peer(k)).wait_recv()

    tile_f = min(128, F)

    def weight_step(m):
        rows = pl.ds(pl.multiple_of(m * tile_f, tile_f), tile_f)
        both = dot(ytbuf[rows, :], ggbuf[...].reshape(tokens, 2 * H)).astype(jnp.bfloat16)
        dg_ref[rows, :] = both[:, 0:H]
        du_ref[rows, :] = both[:, H:2 * H]

    loop(F // tile_f, weight_step)

    @pl.when(jnp.logical_not(diagonal))
    def _():
        go_copy.wait_recv()
    gval_ref[...] = gvrecv[...]

    for j in range(YH):
        @pl.when(jnp.logical_not(diagonal & (yh == j)))
        def _():
            first_copy(j).wait_send()

    @pl.when(jnp.logical_not(diagonal))
    def _():
        gv_copy.wait_send()
        go_copy.wait_send()

    def row_sends(k):
        q = row_peer(k)
        t1_copy(k).wait_send()
        rs_copy(q).wait_send()
        q1_copy(q).wait_send()
        h_copy(q).wait_send()
        q2_copy(q).wait_send()
        gh_copy(q).wait_send()
        gg_copy(q).wait_send()

    loop(R, row_sends, 1)

    def depth_sends(k):
        t2_copy(k).wait_send()
        z_copy(k).wait_send()
        a_copy(k).wait_send()
        oz_copy(depth_peer(k)).wait_send()

    loop(Z, depth_sends, 1)

    def pair_sends(k):
        s_copy(k).wait_send()
        as_copy(k).wait_send()
        ob_copy(k).wait_send()

    loop(Z, pair_sends)

    def y_sends(k):
        oy_copy(y_peer(k)).wait_send()
        ay_copy(y_peer(k)).wait_send()

    loop(YH, y_sends, 1)


def build(mesh):
    R, C, Z = mesh.shape["row"], mesh.shape["col"], mesh.shape["depth"]
    YH = C // 2

    def per_device(residual, pre_gain, w_gate, w_up, w_down, value_head, sample_index, return_table):
        B, F = residual.shape
        H = w_gate.shape[1]
        T = C * B
        r = lax.axis_index("row")
        d = lax.axis_index("depth")
        lane = (r % 2) * (YH * B) + (r // 2) * B
        target = jnp.take(return_table, sample_index)
        rows = max(8, Z)
        tile = lax.dynamic_update_slice(
            jnp.zeros((rows, T), jnp.float32), target[None, :], (d, lane)
        )
        gv = jnp.zeros((8, F), jnp.float32).at[0].set(pre_gain).at[1].set(value_head)

        bf, f32 = jnp.bfloat16, jnp.float32
        V = pltpu.VMEM
        dma = lambda *shape: pltpu.SemaphoreType.DMA(shape)
        half = YH * B
        scratch = [
            V((Z, T, F), bf), V((Z, T, F), bf), V((F, Z * T), bf),
            V((R, T, 2 * H), bf), V((R, T, 2 * H), bf), V((T, 2 * H), f32),
            V((R, 8, T), f32), V((R, 8, T), f32),
            V((R, T, H), bf), V((H, R * T), bf),
            V((T, H), f32), V((T, H), f32), V((T, 1), f32),
            V((Z, T, F), bf), V((Z, half, F), bf), V((half, F), f32),
            V((Z, half, F), bf), V((Z, half, F), bf), V((half, F), bf), V((YH, B, F), bf),
            V((Z, T, F), bf),
            V((2 * Z, T), f32), V((R, 2 * Z, T), f32), V((Z, T), f32), V((Z, T), f32),
            V((Z, T, F), bf), V((R, T, H), bf), V((R, T, H), bf), V((T, H), f32),
            V((R, T, 2 * H), bf),
            V((8, F), f32), V((8, F), f32), V((8, F), f32),
            V((R, rows, T), f32), V((rows, T), f32), V((Z, rows, T), f32),
            dma(YH), dma(YH), dma(), dma(), dma(R), dma(R), dma(Z), dma(Z),
            dma(Z), dma(Z), dma(Z), dma(Z), dma(R), dma(R), dma(R), dma(R), dma(R), dma(R),
            dma(Z), dma(Z), dma(Z), dma(Z), dma(YH), dma(YH), dma(YH), dma(YH),
            dma(Z), dma(Z), dma(Z), dma(Z),
            dma(R), dma(R), dma(R), dma(R), dma(R), dma(R), dma(), dma(),
        ]
        vmem = pl.BlockSpec(memory_space=pltpu.VMEM)
        dg, du, dd, values, gval = pl.pallas_call(
            functools.partial(kernel, R, YH, Z, B, F, H),
            out_shape=(
                jax.ShapeDtypeStruct((F, H), bf),
                jax.ShapeDtypeStruct((F, H), bf),
                jax.ShapeDtypeStruct((H, F), bf),
                jax.ShapeDtypeStruct((Z, T), f32),
                jax.ShapeDtypeStruct((8, F), f32),
            ),
            in_specs=[vmem] * 6,
            out_specs=(vmem,) * 5,
            scratch_shapes=scratch,
            compiler_params=pltpu.CompilerParams(
                collective_id=0, has_side_effects=True, vmem_limit_bytes=40 * 1024 * 1024
            ),
        )(residual, gv, tile, w_gate, w_up, w_down)
        values = lax.dynamic_slice(values, (d, lane), (1, B))[0]
        return values, dg, du, dd, gval[0]

    return per_device


def solution(mesh):
    placed = (
        P(("row", "depth"), "col"),
        P("col"),
        P("row", ("col", "depth")),
        P("row", ("col", "depth")),
        P(("col", "depth"), "row"),
        P("col"),
        P(("row", "depth")),
        P(),
    )
    return jax.shard_map(
        build(mesh),
        mesh=mesh,
        in_specs=placed,
        out_specs=(
            P(("row", "depth")),
            P("row", ("col", "depth")),
            P("row", ("col", "depth")),
            P(("col", "depth"), "row"),
            P("col"),
        ),
        check_vma=False,
    )
```

```python
import functools

import jax
import jax.numpy as jnp
from jax import lax
from jax.experimental import pallas as pl
from jax.experimental.pallas import tpu as pltpu
from jax.sharding import PartitionSpec as P

MESH = pl.DeviceIdType.MESH
norm_eps = 1e-06
huber_delta = 1.0


def rem(value, size):
    return lax.rem(value, jnp.int32(size))


def dot(left, right):
    return jnp.dot(left, right, preferred_element_type=jnp.float32)


def dot_t(left, right):
    return lax.dot_general(
        left, right, (((1,), (1,)), ((), ())), preferred_element_type=jnp.float32
    )


def kernel(
    R, YH, Z, B, F, H,
    x_ref, gv_ref, tgt_ref, wg_ref, wu_ref, wd_ref,
    dg_ref, du_ref, dd_ref, val_ref, gval_ref,
    xbuf, ybuf, y2buf, y2t, wgbuf, wubuf, wdbuf, gvbuf, tg1, tgsend, tg2,
    acc, rssend, rsrecv, st1send, st1recv, hbuf, ht, gubuf, coef,
    osend, osib, oown, zsend, zrecv, ysend, yrecv, outblk, obuf,
    st2send, st2recv, gobuf, go2buf, ghpart, ghsend, ghrecv, ghbuf, ggbuf, gsum, grecv,
    x1s, x1r, x2s, x2r, x3s, x3r, gvs, gvr, gbs, gbr, t1s, t1r, t2s, t2r,
    wls, wgs, wgr, wus, wur, wds, wdr, q1s, q1r, rss, rsr, y2s, y2r, hs, hr, gus, gur,
    obs, obr, ozs, ozr, oys, oyr, a1s, a1r, a2s, a2r, a3s, a3r, q2s, q2r,
    gos, gor, g1s, g1r, ghs, ghr, gvos, gvor,
):
    XN, YQ = R // 2, YH // 2
    N = Z * 2 * B
    L = N // 2
    features = R * F
    r = lax.axis_index("row")
    c = lax.axis_index("col")
    d = lax.axis_index("depth")
    x = rem(r, XN)
    yl = lax.div(r, jnp.int32(XN))
    core = rem(c, 2)
    yh = lax.div(c, jnp.int32(2))
    side = lax.div(yh, jnp.int32(YQ))
    mloc = rem(yh, YQ)
    home = yl == side
    sibling = (r, 2 * yh + 1 - core, d)
    ypair = ((1 - yl) * XN + x, c, d)

    def copy(src, dst, send, recv, device):
        return pltpu.make_async_remote_copy(
            src_ref=src, dst_ref=dst, send_sem=send, recv_sem=recv,
            device_id=device, device_id_type=MESH,
        )

    def row_peer(k):
        return rem(r + k, R)

    def depth_peer(k):
        return rem(d + k, Z)

    def x_peer(k):
        return rem(x + k, XN)

    def row_device(q):
        return (q, c, d)

    def depth_device(q):
        return (r, c, q)

    def x_device(q):
        return (yl * XN + q, c, d)

    def seat(q):
        return rem(q, XN) * 2 + lax.div(q, jnp.int32(XN))

    my_seat = x * 2 + yl

    def reader(j):
        return (side * XN + x, 2 * j + core, d)

    def owner(s, m):
        return (s * XN + x, 2 * (yl * YQ + m) + core, d)

    def is_owner(s, m):
        return (yl == s) & (yh == yl * YQ + m)

    def span(index, size):
        return pl.ds(pl.multiple_of(index * size, size), size)

    def block(depth, s):
        return pl.ds(pl.multiple_of(depth * (2 * B) + s * B, B), B)

    def loop(count, body, start=0):
        def step(k, carry):
            body(k)
            return carry
        lax.fori_loop(start, count, step, 0)

    eye = (
        lax.broadcasted_iota(jnp.int32, (L, L), 0)
        == lax.broadcasted_iota(jnp.int32, (L, L), 1)
    )

    def to_lanes(column):
        return jnp.sum(jnp.where(eye, column, 0.0), axis=0, keepdims=True)

    def to_column(lanes):
        return jnp.sum(jnp.where(eye, lanes, 0.0), axis=1, keepdims=True)

    barrier = pltpu.get_barrier_semaphore()

    def greet(device):
        pl.semaphore_signal(barrier, inc=1, device_id=device, device_id_type=MESH)

    for k in range(1, R):
        greet(row_device(row_peer(k)))
    for k in range(1, Z):
        greet(depth_device(depth_peer(k)))
    greet(sibling)
    for j in range(YH):
        @pl.when(jnp.logical_not(home & (yh == j)))
        def _():
            greet(reader(j))
    for s in range(2):
        for m in range(YQ):
            @pl.when(jnp.logical_not(is_owner(s, m)))
            def _():
                greet(owner(s, m))
    pl.semaphore_wait(
        barrier, (R - 1) + (Z - 1) + 1 + YH + 2 * YQ - jnp.where(home, 2, 0)
    )

    near = []
    for k in range(1, Z // 2 + 1):
        near.append(k)
        if Z - k > k:
            near.append(Z - k)

    class Gather:
        def __init__(self, src, buf, s1, r1, s2, r2, s3, r3):
            self.src, self.buf = src, buf
            self.sems = (s1, r1, s2, r2, s3, r3)

        def first(self, j):
            s1, r1 = self.sems[:2]
            return copy(
                self.src, self.buf.at[core, mloc, block(d, yl)],
                s1.at[j], r1.at[yl * YQ + mloc], reader(j),
            )

        def first_arrival(self, s, m):
            s1, r1 = self.sems[:2]
            return copy(
                self.src, self.buf.at[core, m, block(d, s)],
                s1.at[0], r1.at[s * YQ + m], owner(s, m),
            )

        def start(self):
            for j in range(YH):
                @pl.when(home & (yh == j))
                def _():
                    self.buf[core, mloc, block(d, yl)] = self.src[...]

                @pl.when(jnp.logical_not(home & (yh == j)))
                def _():
                    self.first(j).start()

        def piece(self, which, q):
            return self.buf.at[which, :, span(q, 2 * B)]

        def z_copy(self, k):
            part = self.piece(core, d)
            return copy(
                part, part, self.sems[2].at[k], self.sems[3].at[k],
                depth_device(depth_peer(k)),
            )

        def z_arrival(self, k):
            q = depth_peer(Z - k)
            part = self.piece(core, q)
            return copy(part, part, self.sems[2].at[k], self.sems[3].at[k], depth_device(q))

        def s_copy(self, k):
            part = self.piece(core, depth_peer(Z - k))
            return copy(part, part, self.sems[4].at[k], self.sems[5].at[k], sibling)

        def s_arrival(self, k):
            part = self.piece(1 - core, depth_peer(Z - k))
            return copy(part, part, self.sems[4].at[k], self.sems[5].at[k], sibling)

        def spread(self):
            for s in range(2):
                for m in range(YQ):
                    @pl.when(jnp.logical_not(is_owner(s, m)))
                    def _():
                        self.first_arrival(s, m).wait_recv()
            for k in near:
                self.z_copy(k).start()
            self.s_copy(0).start()

        def pass_on(self):
            for k in near:
                self.z_arrival(k).wait_recv()
                self.s_copy(k).start()

        def arrived(self):
            for k in [0] + near:
                self.s_arrival(k).wait_recv()

        def drain(self):
            for j in range(YH):
                @pl.when(jnp.logical_not(home & (yh == j)))
                def _():
                    self.first(j).wait_send()
            for k in range(1, Z):
                self.z_copy(k).wait_send()
            for k in range(Z):
                self.s_copy(k).wait_send()

    gx = Gather(x_ref, xbuf, x1s, x1r, x2s, x2r, x3s, x3r)
    gx.start()

    def gv_copy(j):
        return copy(gv_ref, gvbuf.at[core, mloc], gvs.at[j], gvr.at[mloc], reader(j))

    def gv_arrival(m):
        return copy(gv_ref, gvbuf.at[core, m], gvs.at[0], gvr.at[m], owner(0, m))

    for j in range(YH):
        @pl.when((yl == 0) & home & (yh == j))
        def _():
            gvbuf[core, mloc] = gv_ref[...]

        @pl.when((yl == 0) & jnp.logical_not(home & (yh == j)))
        def _():
            gv_copy(j).start()

    def local_weights():
        return (
            pltpu.make_async_copy(wg_ref, wgbuf.at[x], wls.at[0]),
            pltpu.make_async_copy(wu_ref, wubuf.at[x], wls.at[1]),
            pltpu.make_async_copy(wd_ref, wdbuf.at[x], wls.at[2]),
        )

    for one in local_weights():
        one.start()

    def w_copy(ref, buf, send, recv, k):
        return copy(ref, buf.at[x], send.at[k], recv.at[k], x_device(x_peer(k)))

    def w_arrival(ref, buf, send, recv, k):
        q = x_peer(XN - k)
        return copy(ref, buf.at[q], send.at[k], recv.at[k], x_device(q))

    gate_w = (wg_ref, wgbuf, wgs, wgr)
    up_w = (wu_ref, wubuf, wus, wur)
    down_w = (wd_ref, wdbuf, wds, wdr)
    for k in range(1, XN):
        w_copy(*gate_w, k).start()
        w_copy(*up_w, k).start()

    t1_copy = copy(tgt_ref, tg1, t1s, t1r, ypair)
    t1_copy.start()

    gx.spread()

    for m in range(YQ):
        @pl.when(jnp.logical_not((yl == 0) & is_owner(0, m)))
        def _():
            gv_arrival(m).wait_recv()
    gb_copy = copy(gvbuf.at[core], gvbuf.at[core], gbs, gbr, sibling)
    gb_arrival = copy(gvbuf.at[1 - core], gvbuf.at[1 - core], gbs, gbr, sibling)
    gb_copy.start()

    t1_copy.wait_recv()
    tgsend[...] = tgt_ref[...] + tg1[...]

    def t2_copy(k):
        return copy(tgsend, tg2.at[d], t2s.at[k], t2r.at[k], depth_device(depth_peer(k)))

    def t2_arrival(k):
        q = depth_peer(Z - k)
        return copy(tgsend, tg2.at[q], t2s.at[k], t2r.at[k], depth_device(q))

    for k in range(1, Z):
        t2_copy(k).start()

    gx.pass_on()

    for one in local_weights():
        one.wait()
    for k in range(1, XN):
        w_arrival(*gate_w, k).wait_recv()
        w_arrival(*up_w, k).wait_recv()
    for k in range(1, XN):
        w_copy(*down_w, k).start()

    def gate_up(which, m):
        fl = 2 * m + which
        wide = xbuf[which, m].astype(jnp.float32)
        scaled = (wide * gvbuf[which, m, 0:1, :]).astype(jnp.bfloat16)
        ybuf[fl] = scaled
        acc[:, 0:H] += dot(scaled, wgbuf[fl])
        acc[:, H:2 * H] += dot(scaled, wubuf[fl])
        squares = jnp.sum(wide * wide, axis=1, keepdims=True)
        for s in range(2):
            st1send[s:s + 1, :] += to_lanes(squares[s * L:(s + 1) * L])

    acc[...] = jnp.zeros_like(acc)
    st1send[...] = jnp.zeros_like(st1send)
    loop(YQ, lambda m: gate_up(core, m))
    gb_arrival.wait_recv()
    gx.arrived()
    loop(YQ, lambda m: gate_up(1 - core, m))

    rs_copy = copy(rssend, rsrecv, rss, rsr, ypair)
    rssend[...] = acc[span(1 - yl, L)].astype(jnp.bfloat16)

    def q1_copy(q):
        return copy(st1send, st1recv.at[r], q1s.at[q], q1r.at[r], row_device(q))

    def q1_arrival(q):
        return copy(st1send, st1recv.at[q], q1s.at[q], q1r.at[q], row_device(q))

    pair_row = (1 - yl) * XN + x
    q1_copy(pair_row).start()
    rs_copy.start()
    for k in range(1, R):
        q = row_peer(k)

        @pl.when(q != pair_row)
        def _():
            q1_copy(q).start()
    st1recv[r] = st1send[...]

    def y2_copy(k):
        q = x_peer(k)
        return copy(ybuf.at[q], y2buf.at[x], y2s.at[k], y2r.at[k], x_device(q))

    def y2_arrival(k):
        q = x_peer(XN - k)
        return copy(ybuf.at[x], y2buf.at[q], y2s.at[k], y2r.at[k], x_device(q))

    for k in range(1, XN):
        y2_copy(k).start()

    q1_arrival(pair_row).wait_recv()
    squares = st1send[...] + st1recv[pair_row]
    inv_lanes = lax.rsqrt(squares / features + norm_eps)
    inv_mine = jnp.where(yl == 0, inv_lanes[0:1, :], inv_lanes[1:2, :])
    inv_norm = to_column(inv_mine)
    rs_copy.wait_recv()
    total = (acc[span(yl, L)] + rsrecv[...].astype(jnp.float32)) * inv_norm
    gate, up = total[:, 0:H], total[:, H:2 * H]
    hbuf[my_seat] = (gate * jax.nn.sigmoid(gate) * up).astype(jnp.bfloat16)

    def h_copy(q):
        part = hbuf.at[my_seat]
        return copy(part, part, hs.at[q], hr.at[r], row_device(q))

    def h_arrival(q):
        part = hbuf.at[seat(q)]
        return copy(part, part, hs.at[q], hr.at[q], row_device(q))

    def gu_copy(q):
        part = gubuf.at[my_seat]
        return copy(part, part, gus.at[q], gur.at[r], row_device(q))

    def gu_arrival(q):
        part = gubuf.at[seat(q)]
        return copy(part, part, gus.at[q], gur.at[q], row_device(q))

    h_copy(pair_row).start()
    gubuf[my_seat] = total.astype(jnp.bfloat16)

    for k in range(1, XN):
        w_arrival(*down_w, k).wait_recv()

    def ob_copy(s):
        part = pl.ds(pl.multiple_of(s * L, L), L)
        return copy(osend.at[:, part], osib.at[:, part], obs.at[s], obr.at[s], sibling)

    def down(s):
        rows = span(s, L)
        act = hbuf[x * 2 + s]
        for m in range(YQ):
            osend[m, rows] = dot(act, wdbuf[2 * m + 1 - core]).astype(jnp.bfloat16)
        ob_copy(s).start()
        for m in range(YQ):
            oown[m, rows] = dot(act, wdbuf[2 * m + core])

    down(yl)
    for k in range(1, R):
        q = row_peer(k)

        @pl.when(q != pair_row)
        def _():
            h_copy(q).start()
        gu_copy(q).start()

    def oz_copy(q):
        return copy(
            zsend.at[:, span(q, 2 * B)], zrecv.at[d], ozs.at[q], ozr.at[d], depth_device(q)
        )

    def oz_arrival(q):
        return copy(
            zsend.at[:, span(q, 2 * B)], zrecv.at[q], ozs.at[q], ozr.at[q], depth_device(q)
        )

    def pair_sum(s):
        rows = span(s, L)
        ob_copy(s).wait_recv()
        for m in range(YQ):
            both = oown[m, rows] + osib[m, rows].astype(jnp.float32)
            oown[m, rows] = both
            zsend[m, rows] = both.astype(jnp.bfloat16)
        for i in range(Z // 2):
            q = s * (Z // 2) + rem(d + i, Z // 2)

            @pl.when(q != d)
            def _():
                oz_copy(q).start()

    pair_sum(yl)
    h_arrival(pair_row).wait_recv()
    down(1 - yl)
    pair_sum(1 - yl)

    y2buf[x] = ybuf[x]
    y2t[:, span(x, N)] = ybuf[x].T
    for k in range(1, XN):
        q = x_peer(XN - k)
        y2_arrival(k).wait_recv()
        y2t[:, span(q, N)] = y2buf[q].T

    mine = span(d, 2 * B)
    for k in near:
        q = depth_peer(k)
        oz_arrival(q).wait_recv()
        for m in range(YQ):
            oown[m, mine] += zrecv[q, m].astype(jnp.float32)
    for m in range(YQ):
        ysend[m] = oown[m, mine].astype(jnp.bfloat16)

    def oy_copy(s, m):
        return copy(
            ysend.at[m, pl.ds(s * B, B)], yrecv.at[yh], oys.at[s * YQ + m], oyr.at[yh],
            owner(s, m),
        )

    def oy_arrival(j):
        return copy(ysend.at[0, pl.ds(0, B)], yrecv.at[j], oys.at[0], oyr.at[j], reader(j))

    for s in range(2):
        for m in range(YQ):
            @pl.when(is_owner(s, m))
            def _():
                yrecv[yh] = ysend[m, s * B:(s + 1) * B]

            @pl.when(jnp.logical_not(is_owner(s, m)))
            def _():
                oy_copy(s, m).start()
    output = x_ref[...].astype(jnp.float32)
    for j in range(YH):
        @pl.when(jnp.logical_not(home & (yh == j)))
        def _():
            oy_arrival(j).wait_recv()
        output = output + yrecv[j].astype(jnp.float32)
    outblk[...] = output.astype(jnp.bfloat16)

    ga = Gather(outblk, obuf, a1s, a1r, a2s, a2r, a3s, a3r)
    ga.start()

    ht[:, span(my_seat, L)] = hbuf[my_seat].T

    def hidden_step(k):
        q = row_peer(k)

        @pl.when(q != pair_row)
        def _():
            h_arrival(q).wait_recv()
        ht[:, span(seat(q), L)] = hbuf[seat(q)].T

    loop(R, hidden_step, 1)

    ga.spread()

    def coef_of(q):
        s = seat(q)
        first = rem(q, XN)
        parity = lax.div(q, jnp.int32(XN))
        sums = st1recv[first] + st1recv[first + XN]
        lanes = jnp.where(parity == 0, sums[0:1, :], sums[1:2, :])
        inv = to_column(lax.rsqrt(lanes / features + norm_eps))
        both = gubuf[s].astype(jnp.float32)
        gate, up = both[:, 0:H], both[:, H:2 * H]
        sig = jax.nn.sigmoid(gate)
        coef[s, :, 0:H] = inv * (up * sig * (1.0 + gate * (1.0 - sig)))
        coef[s, :, H:2 * H] = inv * (gate * sig)

    for k in range(1, R):
        q = row_peer(k)

        @pl.when(q != pair_row)
        def _():
            q1_arrival(q).wait_recv()

    def coef_step(k):
        q = row_peer(k)
        gu_arrival(q).wait_recv()
        coef_of(q)

    loop(R, coef_step, 1)
    coef_of(r)

    ga.pass_on()

    target = tgsend[...]
    for k in range(1, Z):
        t2_arrival(k).wait_recv()
        target = target + tg2[depth_peer(Z - k)]

    def stats(which, m):
        wide = obuf[which, m].astype(jnp.float32)
        head = gvbuf[which, m, 1:2, :]
        squares = jnp.sum(wide * wide, axis=1, keepdims=True)
        products = jnp.sum(wide * head, axis=1, keepdims=True)
        for s in range(2):
            part = slice(s * L, (s + 1) * L)
            st2send[s:s + 1, :] += to_lanes(squares[part])
            st2send[2 + s:3 + s, :] += to_lanes(products[part])

    st2send[...] = jnp.zeros_like(st2send)
    loop(YQ, lambda m: stats(core, m))
    ga.arrived()
    loop(YQ, lambda m: stats(1 - core, m))
    q2_copy = copy(st2send, st2recv, q2s, q2r, ypair)
    q2_copy.start()
    q2_copy.wait_recv()
    sums = st2send[...] + st2recv[...]
    inv_final = lax.rsqrt(sums[0:2] / features + norm_eps)
    values = sums[2:4] * inv_final
    val_ref[...] = jnp.broadcast_to(values[None], (4, 2, L)).reshape(8, L)
    slope = jnp.clip(values - target[0:2], -huber_delta, huber_delta)
    scale_lanes = inv_final * slope
    shrink_lanes = inv_final * inv_final * (slope * values / features)
    scale = jnp.concatenate([to_column(scale_lanes[s:s + 1]) for s in range(2)], axis=0)
    shrink = jnp.concatenate([to_column(shrink_lanes[s:s + 1]) for s in range(2)], axis=0)

    def go_copy(k):
        q = x_peer(k)
        return copy(gobuf.at[q], go2buf.at[x], gos.at[k], gor.at[k], x_device(q))

    def go_arrival(k):
        q = x_peer(XN - k)
        return copy(gobuf.at[x], go2buf.at[q], gos.at[k], gor.at[k], x_device(q))

    gsum[...] = jnp.zeros_like(gsum)
    ghpart[...] = jnp.zeros_like(ghpart)

    def grad_output(fl):
        which = rem(fl, 2)
        m = lax.div(fl, jnp.int32(2))
        wide = obuf[which, m].astype(jnp.float32)
        head = gvbuf[which, m, 1:2, :]
        gobuf[fl] = (scale * head - shrink * wide).astype(jnp.bfloat16)
        gsum[pl.ds(fl, 1), :] = jnp.sum(wide * scale, axis=0, keepdims=True)
        ghpart[...] += dot_t(gobuf[fl], wdbuf[fl])

    loop(XN, grad_output)

    g1_copy = copy(ghsend, ghrecv, g1s, g1r, ypair)
    ghsend[...] = ghpart[span(1 - yl, L)].astype(jnp.bfloat16)
    g1_copy.start()
    for k in range(1, XN):
        go_copy(k).start()

    def gvo_copy(q):
        return copy(gsum, grecv.at[r], gvos.at[q], gvor.at[r], row_device(q))

    def gvo_arrival(q):
        return copy(gsum, grecv.at[q], gvos.at[q], gvor.at[q], row_device(q))

    def gh_copy(q):
        part = ghbuf.at[my_seat]
        return copy(part, part, ghs.at[q], ghr.at[r], row_device(q))

    def gh_arrival(q):
        part = ghbuf.at[seat(q)]
        return copy(part, part, ghs.at[q], ghr.at[q], row_device(q))

    go2buf[x] = gobuf[x]
    g1_copy.wait_recv()
    ghbuf[my_seat] = (
        ghpart[span(yl, L)] + ghrecv[...].astype(jnp.float32)
    ).astype(jnp.bfloat16)
    for k in range(1, R):
        gh_copy(row_peer(k)).start()
    for k in range(1, R):
        gvo_copy(row_peer(k)).start()
    grecv[r] = gsum[...]

    for k in range(1, XN):
        go_arrival(k).wait_recv()
    tokens = XN * N
    tile = min(128, H)

    def down_weight_step(i):
        rows = span(i, tile)
        dd_ref[rows, :] = dot(ht[rows, :], go2buf[...].reshape(tokens, F)).astype(jnp.bfloat16)

    loop(H // tile, down_weight_step)

    def gg_of(s):
        grad = ghbuf[s].astype(jnp.float32)
        ggbuf[s, :, 0:H] = (grad * coef[s, :, 0:H]).astype(jnp.bfloat16)
        ggbuf[s, :, H:2 * H] = (grad * coef[s, :, H:2 * H]).astype(jnp.bfloat16)

    gg_of(my_seat)

    def gg_step(k):
        q = row_peer(k)
        gh_arrival(q).wait_recv()
        gg_of(seat(q))

    loop(R, gg_step, 1)

    tile_f = min(128, F)

    def weight_step(i):
        rows = span(i, tile_f)
        both = dot(y2t[rows, :], ggbuf[...].reshape(tokens, 2 * H)).astype(jnp.bfloat16)
        dg_ref[rows, :] = both[:, 0:H]
        du_ref[rows, :] = both[:, H:2 * H]

    loop(F // tile_f, weight_step)

    for k in range(1, R):
        gvo_arrival(row_peer(k)).wait_recv()
    head_sum = grecv[side * XN]
    for k in range(1, XN):
        head_sum = head_sum + grecv[side * XN + k]
    pick = lax.broadcasted_iota(jnp.int32, head_sum.shape, 0) == c - side * XN
    gval_ref[...] = jnp.broadcast_to(
        jnp.sum(jnp.where(pick, head_sum, 0.0), axis=0, keepdims=True), gval_ref.shape
    )

    gx.drain()
    ga.drain()
    for j in range(YH):
        @pl.when((yl == 0) & jnp.logical_not(home & (yh == j)))
        def _():
            gv_copy(j).wait_send()
    gb_copy.wait_send()
    t1_copy.wait_send()
    rs_copy.wait_send()
    q2_copy.wait_send()
    g1_copy.wait_send()

    def x_sends(k):
        w_copy(*gate_w, k).wait_send()
        w_copy(*up_w, k).wait_send()
        w_copy(*down_w, k).wait_send()
        y2_copy(k).wait_send()
        go_copy(k).wait_send()

    loop(XN, x_sends, 1)

    def row_sends(k):
        q = row_peer(k)
        q1_copy(q).wait_send()
        h_copy(q).wait_send()
        gu_copy(q).wait_send()
        gh_copy(q).wait_send()
        gvo_copy(q).wait_send()

    loop(R, row_sends, 1)

    def depth_sends(k):
        t2_copy(k).wait_send()
        oz_copy(depth_peer(k)).wait_send()

    loop(Z, depth_sends, 1)
    for s in range(2):
        ob_copy(s).wait_send()
        for m in range(YQ):
            @pl.when(jnp.logical_not(is_owner(s, m)))
            def _():
                oy_copy(s, m).wait_send()


def build(mesh):
    R, C, Z = mesh.shape["row"], mesh.shape["col"], mesh.shape["depth"]
    YH, XN = C // 2, R // 2
    YQ = YH // 2

    def per_device(residual, pre_gain, w_gate, w_up, w_down, value_head, sample_index, return_table):
        B, F = residual.shape
        H = w_gate.shape[1]
        N = Z * 2 * B
        L = N // 2
        r = lax.axis_index("row")
        d = lax.axis_index("depth")
        place = d * (2 * B) + (r // XN) * B
        target = jnp.take(return_table, sample_index)
        tile = lax.dynamic_update_slice(
            jnp.zeros((8, L), jnp.float32), target[None, :], (place // L, place % L)
        )
        gv = jnp.zeros((8, F), jnp.float32).at[0].set(pre_gain).at[1].set(value_head)

        bf, f32 = jnp.bfloat16, jnp.float32
        V = pltpu.VMEM
        dma = lambda *shape: pltpu.SemaphoreType.DMA(shape)
        scratch = [
            V((2, YQ, N, F), bf), V((XN, N, F), bf), V((XN, N, F), bf), V((F, XN * N), bf),
            V((XN, F, H), bf), V((XN, F, H), bf), V((XN, H, F), bf),
            V((2, YQ, 8, F), f32), V((8, L), f32), V((8, L), f32), V((Z, 8, L), f32),
            V((N, 2 * H), f32), V((L, 2 * H), bf), V((L, 2 * H), bf),
            V((8, L), f32), V((R, 8, L), f32),
            V((R, L, H), bf), V((H, R * L), bf), V((R, L, 2 * H), bf), V((R, L, 2 * H), f32),
            V((YQ, N, F), bf), V((YQ, N, F), bf), V((YQ, N, F), f32),
            V((YQ, N, F), bf), V((Z, YQ, 2 * B, F), bf), V((YQ, 2 * B, F), bf), V((YH, B, F), bf),
            V((B, F), bf), V((2, YQ, N, F), bf),
            V((8, L), f32), V((8, L), f32),
            V((XN, N, F), bf), V((XN, N, F), bf), V((N, H), f32), V((L, H), bf), V((L, H), bf),
            V((R, L, H), bf), V((R, L, 2 * H), bf), V((8, F), f32), V((R, 8, F), f32),
            dma(YH), dma(2 * YQ), dma(Z), dma(Z), dma(Z), dma(Z),
            dma(YH), dma(YQ), dma(), dma(), dma(), dma(), dma(Z), dma(Z),
            dma(3), dma(XN), dma(XN), dma(XN), dma(XN), dma(XN), dma(XN),
            dma(R), dma(R), dma(), dma(), dma(XN), dma(XN), dma(R), dma(R), dma(R), dma(R),
            dma(2), dma(2), dma(Z), dma(Z), dma(2 * YQ), dma(YH),
            dma(YH), dma(2 * YQ), dma(Z), dma(Z), dma(Z), dma(Z), dma(), dma(),
            dma(XN), dma(XN), dma(), dma(), dma(R), dma(R), dma(R), dma(R),
        ]
        vmem = pl.BlockSpec(memory_space=pltpu.VMEM)
        hbm = pl.BlockSpec(memory_space=pl.ANY)
        dg, du, dd, values, gval = pl.pallas_call(
            functools.partial(kernel, R, YH, Z, B, F, H),
            out_shape=(
                jax.ShapeDtypeStruct((F, H), bf),
                jax.ShapeDtypeStruct((F, H), bf),
                jax.ShapeDtypeStruct((H, F), bf),
                jax.ShapeDtypeStruct((8, L), f32),
                jax.ShapeDtypeStruct((8, F), f32),
            ),
            in_specs=[vmem, vmem, vmem, hbm, hbm, hbm],
            out_specs=(vmem,) * 5,
            scratch_shapes=scratch,
            compiler_params=pltpu.CompilerParams(
                collective_id=0, has_side_effects=True, vmem_limit_bytes=40 * 1024 * 1024
            ),
        )(residual, gv, tile, w_gate, w_up, w_down)
        values = lax.dynamic_slice(values, (place // L, place % L), (1, B))[0]
        return values, dg, du, dd, gval[0]

    return per_device


def solution(mesh):
    placed = (
        P(("row", "depth"), "col"),
        P("col"),
        P("row", ("col", "depth")),
        P("row", ("col", "depth")),
        P(("col", "depth"), "row"),
        P("col"),
        P(("row", "depth")),
        P(),
    )
    return jax.shard_map(
        build(mesh),
        mesh=mesh,
        in_specs=placed,
        out_specs=(
            P(("row", "depth")),
            P("row", ("col", "depth")),
            P("row", ("col", "depth")),
            P(("col", "depth"), "row"),
            P("col"),
        ),
        check_vma=False,
    )
```

```python
import functools

import jax
import jax.numpy as jnp
from jax import lax
from jax.experimental import pallas as pl
from jax.experimental.pallas import tpu as pltpu
from jax.sharding import PartitionSpec as P

MESH = pl.DeviceIdType.MESH
norm_eps = 1e-06
huber_delta = 1.0


def rem(value, size):
    return lax.rem(value, jnp.int32(size))


def dot(left, right):
    return jnp.dot(left, right, preferred_element_type=jnp.float32)


def dot_t(left, right):
    return lax.dot_general(
        left, right, (((1,), (1,)), ((), ())), preferred_element_type=jnp.float32
    )


def kernel(
    R, YH, Z, B, F, H,
    x_ref, gv_ref, tgt_ref, wg_ref, wu_ref, wd_ref,
    dg_ref, du_ref, dd_ref, val_ref, gval_ref,
    xbuf, xzb, ybuf, y2buf, y2t, wgbuf, wubuf, wdbuf, gvbuf, tg1, tgsend, tg2,
    acc, rssend, rsrecv, st1send, st1recv, hbuf, ht, gubuf, coef,
    osend, osib, oown, zsend, zra, yra, yrb, zrb, ysa, zsb, outblk, obuf, ozb,
    st2send, st2recv, scsend, screcv, o2buf, gobuf, go2buf,
    ghpart, ghsend, ghrecv, ghbuf, ggbuf, gsum, grecv,
    x1, x2, x3, x4, x5, x6, x7, x8, x9, x10, x11, x12, gvs, gvr, gbs, gbr, t1s, t1r, t2s, t2r,
    wls, wgs, wgr, wus, wur, wds, wdr, q1s, q1r, rss, rsr, y2s, y2r, ybs, ybr, hs, hr, gus, gur,
    obs, obr, zas, zar, yas, yar, ybbs, ybbr, zbs, zbr,
    a1, a2, a3, a4, a5, a6, a7, a8, a9, a10, a11, a12, q2s, q2r, scs, scr,
    o2s, o2r, o3s, o3r, g1s, g1r, ghs, ghr, gvos, gvor,
):
    XN, YQ = R // 2, YH // 2
    N = Z * 2 * B
    L = N // 2
    features = R * F
    F2 = F // 2
    ZH = Z // 2
    lo, hi = pl.ds(0, F2), pl.ds(F2, F2)
    r = lax.axis_index("row")
    c = lax.axis_index("col")
    d = lax.axis_index("depth")
    x = rem(r, XN)
    yl = lax.div(r, jnp.int32(XN))
    core = rem(c, 2)
    yh = lax.div(c, jnp.int32(2))
    side = lax.div(yh, jnp.int32(YQ))
    mloc = rem(yh, YQ)
    home = yl == side
    sibling = (r, 2 * yh + 1 - core, d)
    ypair = ((1 - yl) * XN + x, c, d)

    def copy(src, dst, send, recv, device):
        return pltpu.make_async_remote_copy(
            src_ref=src, dst_ref=dst, send_sem=send, recv_sem=recv,
            device_id=device, device_id_type=MESH,
        )

    def row_peer(k):
        return rem(r + k, R)

    def depth_peer(k):
        return rem(d + k, Z)

    def x_peer(k):
        return rem(x + k, XN)

    def row_device(q):
        return (q, c, d)

    def depth_device(q):
        return (r, c, q)

    def x_device(q):
        return (yl * XN + q, c, d)

    def seat(q):
        return rem(q, XN) * 2 + lax.div(q, jnp.int32(XN))

    my_seat = x * 2 + yl

    def reader(j):
        return (side * XN + x, 2 * j + core, d)

    def owner(s, m):
        return (s * XN + x, 2 * (yl * YQ + m) + core, d)

    def is_owner(s, m):
        return (yl == s) & (yh == yl * YQ + m)

    def span(index, size):
        return pl.ds(pl.multiple_of(index * size, size), size)

    def loop(count, body, start=0):
        def step(k, carry):
            body(k)
            return carry
        lax.fori_loop(start, count, step, 0)

    eye = (
        lax.broadcasted_iota(jnp.int32, (L, L), 0)
        == lax.broadcasted_iota(jnp.int32, (L, L), 1)
    )

    def to_lanes(column):
        return jnp.sum(jnp.where(eye, column, 0.0), axis=0, keepdims=True)

    def to_column(lanes):
        return jnp.sum(jnp.where(eye, lanes, 0.0), axis=1, keepdims=True)

    barrier = pltpu.get_barrier_semaphore()

    def greet(device):
        pl.semaphore_signal(barrier, inc=1, device_id=device, device_id_type=MESH)

    for k in range(1, R):
        greet(row_device(row_peer(k)))
    for k in range(1, Z):
        greet(depth_device(depth_peer(k)))
    greet(sibling)
    for j in range(YH):
        @pl.when(jnp.logical_not(home & (yh == j)))
        def _():
            greet(reader(j))
    for s in range(2):
        for m in range(YQ):
            @pl.when(jnp.logical_not(is_owner(s, m)))
            def _():
                greet(owner(s, m))
    pl.semaphore_wait(
        barrier, (R - 1) + (Z - 1) + 1 + YH + 2 * YQ - jnp.where(home, 2, 0)
    )

    near = []
    for k in range(1, Z // 2 + 1):
        near.append(k)
        if Z - k > k:
            near.append(Z - k)

    class Gather:
        def __init__(self, src, buf, zb, *sems):
            self.src, self.buf, self.zb = src, buf, zb
            (self.ays, self.ayr, self.azs, self.azr, self.ass, self.asr,
             self.bzs, self.bzr, self.bys, self.byr, self.bss, self.bsr) = sems

        def ay_copy(self, j):
            return copy(
                self.src.at[:, lo], self.buf.at[core, mloc, d, yl, :, lo],
                self.ays.at[j], self.ayr.at[yl * YQ + mloc], reader(j),
            )

        def ay_arrival(self, s, m):
            return copy(
                self.src.at[:, lo], self.buf.at[core, m, d, s, :, lo],
                self.ays.at[0], self.ayr.at[s * YQ + m], owner(s, m),
            )

        def az_copy(self, k):
            part = self.buf.at[core, :, d, :, :, lo]
            return copy(
                part, part, self.azs.at[k], self.azr.at[k], depth_device(depth_peer(k))
            )

        def az_arrival(self, k):
            q = depth_peer(Z - k)
            part = self.buf.at[core, :, q, :, :, lo]
            return copy(part, part, self.azs.at[k], self.azr.at[k], depth_device(q))

        def as_copy(self, k):
            part = self.buf.at[core, :, depth_peer(Z - k), :, :, lo]
            return copy(part, part, self.ass.at[k], self.asr.at[k], sibling)

        def as_arrival(self, k):
            part = self.buf.at[1 - core, :, depth_peer(Z - k), :, :, lo]
            return copy(part, part, self.ass.at[k], self.asr.at[k], sibling)

        def bz_copy(self, k):
            return copy(
                self.src.at[:, hi], self.zb.at[d], self.bzs.at[k], self.bzr.at[k],
                depth_device(depth_peer(k)),
            )

        def bz_arrival(self, k):
            q = depth_peer(Z - k)
            return copy(
                self.src.at[:, hi], self.zb.at[q], self.bzs.at[k], self.bzr.at[k],
                depth_device(q),
            )

        def by_copy(self, j):
            return copy(
                self.zb, self.buf.at[core, mloc, :, yl, :, hi],
                self.bys.at[j], self.byr.at[yl * YQ + mloc], reader(j),
            )

        def by_arrival(self, s, m):
            return copy(
                self.zb, self.buf.at[core, m, :, s, :, hi],
                self.bys.at[0], self.byr.at[s * YQ + m], owner(s, m),
            )

        def bs_copy(self, s, m):
            part = self.buf.at[core, m, :, s, :, hi]
            i = s * YQ + m
            return copy(part, part, self.bss.at[i], self.bsr.at[i], sibling)

        def bs_arrival(self, s, m):
            part = self.buf.at[1 - core, m, :, s, :, hi]
            i = s * YQ + m
            return copy(part, part, self.bss.at[i], self.bsr.at[i], sibling)

        def start(self):
            for k in reversed(near):
                self.bz_copy(k).start()
            for j in range(YH):
                @pl.when(home & (yh == j))
                def _():
                    self.buf[core, mloc, d, yl, :, 0:F2] = self.src[:, 0:F2]

                @pl.when(jnp.logical_not(home & (yh == j)))
                def _():
                    self.ay_copy(j).start()
            self.zb[d] = self.src[:, F2:F]

        def spread(self):
            for s in range(2):
                for m in range(YQ):
                    @pl.when(jnp.logical_not(is_owner(s, m)))
                    def _():
                        self.ay_arrival(s, m).wait_recv()
            for k in reversed(near):
                self.az_copy(k).start()
            self.as_copy(0).start()
            for k in near:
                self.bz_arrival(k).wait_recv()
            for j in range(YH):
                @pl.when(home & (yh == j))
                def _():
                    self.buf[core, mloc, :, yl, :, F2:F] = self.zb[...]

                @pl.when(jnp.logical_not(home & (yh == j)))
                def _():
                    self.by_copy(j).start()

        def pass_on(self, ks):
            for k in ks:
                self.az_arrival(k).wait_recv()
                self.as_copy(k).start()

        def pass_on_upper(self):
            for s in range(2):
                for m in range(YQ):
                    @pl.when(jnp.logical_not(is_owner(s, m)))
                    def _():
                        self.by_arrival(s, m).wait_recv()
                    self.bs_copy(s, m).start()

        def arrived(self):
            for k in [0] + near:
                self.as_arrival(k).wait_recv()
            for s in range(2):
                for m in range(YQ):
                    self.bs_arrival(s, m).wait_recv()

        def drain(self):
            for j in range(YH):
                @pl.when(jnp.logical_not(home & (yh == j)))
                def _():
                    self.ay_copy(j).wait_send()
                    self.by_copy(j).wait_send()
            for k in range(1, Z):
                self.az_copy(k).wait_send()
                self.bz_copy(k).wait_send()
            for k in range(Z):
                self.as_copy(k).wait_send()
            for s in range(2):
                for m in range(YQ):
                    self.bs_copy(s, m).wait_send()

    gx = Gather(x_ref, xbuf, xzb, x1, x2, x3, x4, x5, x6, x7, x8, x9, x10, x11, x12)
    gx.start()

    def gv_copy(j):
        return copy(gv_ref, gvbuf.at[core, mloc], gvs.at[j], gvr.at[mloc], reader(j))

    def gv_arrival(m):
        return copy(gv_ref, gvbuf.at[core, m], gvs.at[0], gvr.at[m], owner(0, m))

    for j in range(YH):
        @pl.when((yl == 0) & home & (yh == j))
        def _():
            gvbuf[core, mloc] = gv_ref[...]

        @pl.when((yl == 0) & jnp.logical_not(home & (yh == j)))
        def _():
            gv_copy(j).start()

    def local_weights():
        return (
            pltpu.make_async_copy(wg_ref, wgbuf.at[x], wls.at[0]),
            pltpu.make_async_copy(wu_ref, wubuf.at[x], wls.at[1]),
            pltpu.make_async_copy(wd_ref, wdbuf.at[x], wls.at[2]),
        )

    for one in local_weights():
        one.start()

    def w_copy(ref, buf, send, recv, k):
        return copy(ref, buf.at[x], send.at[k], recv.at[k], x_device(x_peer(k)))

    def w_arrival(ref, buf, send, recv, k):
        q = x_peer(XN - k)
        return copy(ref, buf.at[q], send.at[k], recv.at[k], x_device(q))

    def w_onward(ref, buf, send, recv, k):
        rows = ref.shape[0] // 2
        part = buf.at[x_peer(XN - k), pl.ds(0 if k == 1 else rows, rows)]
        return copy(part, part, send.at[k - 1], recv.at[k - 1], x_device(x_peer(k)))

    def w_onward_arrival(ref, buf, send, recv, k):
        rows = ref.shape[0] // 2
        part = buf.at[x_peer(2), pl.ds(0 if k == 1 else rows, rows)]
        return copy(part, part, send.at[k - 1], recv.at[k - 1], x_device(x_peer(XN - k)))

    gate_w = (wg_ref, wgbuf, wgs, wgr)
    up_w = (wu_ref, wubuf, wus, wur)
    down_w = (wd_ref, wdbuf, wds, wdr)
    sides = (1,) if XN == 2 else (1, 3)

    def w_start(*which):
        for k in sides:
            for w in which:
                w_copy(*w, k).start()

    def w_turn(*which):
        for k in sides:
            for w in which:
                w_arrival(*w, k).wait_recv()
                if XN == 4:
                    w_onward(*w, k).start()

    def w_finish(*which):
        if XN == 4:
            for k in sides:
                for w in which:
                    w_onward_arrival(*w, k).wait_recv()

    def w_drain(*which):
        for k in sides:
            for w in which:
                w_copy(*w, k).wait_send()
                if XN == 4:
                    w_onward(*w, k).wait_send()

    w_start(gate_w, up_w)

    t1_copy = copy(tgt_ref, tg1, t1s, t1r, ypair)
    t1_copy.start()

    gx.spread()

    for m in range(YQ):
        @pl.when(jnp.logical_not((yl == 0) & is_owner(0, m)))
        def _():
            gv_arrival(m).wait_recv()
    gb_copy = copy(gvbuf.at[core], gvbuf.at[core], gbs, gbr, sibling)
    gb_arrival = copy(gvbuf.at[1 - core], gvbuf.at[1 - core], gbs, gbr, sibling)
    gb_copy.start()

    t1_copy.wait_recv()
    tgsend[...] = tgt_ref[...] + tg1[...]

    def t2_copy(k):
        return copy(tgsend, tg2.at[d], t2s.at[k], t2r.at[k], depth_device(depth_peer(k)))

    def t2_arrival(k):
        q = depth_peer(Z - k)
        return copy(tgsend, tg2.at[q], t2s.at[k], t2r.at[k], depth_device(q))

    for k in range(1, Z):
        t2_copy(k).start()

    gx.pass_on(near[:5])
    w_turn(gate_w, up_w)
    w_start(down_w)
    gx.pass_on(near[5:])
    gx.pass_on_upper()
    for one in local_weights():
        one.wait()

    def gate_up(which, m):
        fl = 2 * m + which
        wide = xbuf[which, m].reshape(N, F).astype(jnp.float32)
        scaled = (wide * gvbuf[which, m, 0:1, :]).astype(jnp.bfloat16)
        ybuf[fl] = scaled
        acc[:, 0:H] += dot(scaled, wgbuf[fl])
        acc[:, H:2 * H] += dot(scaled, wubuf[fl])
        squares = jnp.sum(wide * wide, axis=1, keepdims=True)
        for s in range(2):
            st1send[s:s + 1, :] += to_lanes(squares[s * L:(s + 1) * L])

    acc[...] = jnp.zeros_like(acc)
    st1send[...] = jnp.zeros_like(st1send)
    w_finish(gate_w, up_w)
    loop(YQ, lambda m: gate_up(core, m))
    w_turn(down_w)
    gb_arrival.wait_recv()
    gx.arrived()
    loop(YQ, lambda m: gate_up(1 - core, m))

    rs_copy = copy(rssend, rsrecv, rss, rsr, ypair)
    rssend[...] = acc[span(1 - yl, L)].astype(jnp.bfloat16)

    def q1_copy(q):
        return copy(st1send, st1recv.at[r], q1s.at[q], q1r.at[r], row_device(q))

    def q1_arrival(q):
        return copy(st1send, st1recv.at[q], q1s.at[q], q1r.at[q], row_device(q))

    pair_row = (1 - yl) * XN + x
    q1_copy(pair_row).start()
    rs_copy.start()
    for k in range(1, R):
        q = row_peer(k)

        @pl.when(q != pair_row)
        def _():
            q1_copy(q).start()
    st1recv[r] = st1send[...]

    near_half = span(core, L)
    far_half = span(1 - core, L)

    def y2_copy(k):
        q = x_peer(k)
        return copy(
            ybuf.at[q, near_half], y2buf.at[x, near_half], y2s.at[k], y2r.at[k], x_device(q)
        )

    def y2_arrival(k):
        q = x_peer(XN - k)
        part = y2buf.at[q, near_half]
        return copy(part, part, y2s.at[k], y2r.at[k], x_device(q))

    def yb_copy(k):
        part = y2buf.at[x_peer(XN - k), near_half]
        return copy(part, part, ybs.at[k], ybr.at[k], sibling)

    def yb_arrival(k):
        part = y2buf.at[x_peer(XN - k), far_half]
        return copy(part, part, ybs.at[k], ybr.at[k], sibling)

    for k in range(1, XN):
        y2_copy(k).start()

    q1_arrival(pair_row).wait_recv()
    squares = st1send[...] + st1recv[pair_row]
    inv_lanes = lax.rsqrt(squares / features + norm_eps)
    inv_mine = jnp.where(yl == 0, inv_lanes[0:1, :], inv_lanes[1:2, :])
    inv_norm = to_column(inv_mine)
    rs_copy.wait_recv()
    total = (acc[span(yl, L)] + rsrecv[...].astype(jnp.float32)) * inv_norm
    gate, up = total[:, 0:H], total[:, H:2 * H]
    hbuf[yl] = (gate * jax.nn.sigmoid(gate) * up).astype(jnp.bfloat16)

    h_copy = copy(hbuf.at[yl], hbuf.at[yl], hs, hr, ypair)
    h_arrival = copy(hbuf.at[1 - yl], hbuf.at[1 - yl], hs, hr, ypair)

    def gu_copy(q):
        part = gubuf.at[my_seat]
        return copy(part, part, gus.at[q], gur.at[r], row_device(q))

    def gu_arrival(q):
        part = gubuf.at[seat(q)]
        return copy(part, part, gus.at[q], gur.at[q], row_device(q))

    h_copy.start()
    gubuf[my_seat] = total.astype(jnp.bfloat16)

    w_finish(down_w)

    def ob_copy(s):
        part = pl.ds(pl.multiple_of(s * L, L), L)
        return copy(osend.at[:, part], osib.at[:, part], obs.at[s], obr.at[s], sibling)

    def down(s):
        rows = span(s, L)
        act = hbuf[s]
        for m in range(YQ):
            osend[m, rows] = dot(act, wdbuf[2 * m + 1 - core]).astype(jnp.bfloat16)
        ob_copy(s).start()
        for m in range(YQ):
            oown[m, rows] = dot(act, wdbuf[2 * m + core])

    down(yl)
    for k in range(1, R):
        gu_copy(row_peer(k)).start()

    def za_copy(q):
        return copy(
            zsend.at[:, q, :, :, lo], zra.at[d], zas.at[q], zar.at[d], depth_device(q)
        )

    def za_arrival(q):
        return copy(
            zsend.at[:, q, :, :, lo], zra.at[q], zas.at[q], zar.at[q], depth_device(q)
        )

    def yb2_copy(s, m):
        return copy(
            zsend.at[m, :, s, :, hi], yrb.at[yh], ybbs.at[s * YQ + m], ybbr.at[yh], owner(s, m)
        )

    def yb2_arrival(j):
        return copy(
            zsend.at[0, :, 0, :, hi], yrb.at[j], ybbs.at[0], ybbr.at[j], reader(j)
        )

    def pair_sum(s):
        rows = span(s, L)
        ob_copy(s).wait_recv()
        for m in range(YQ):
            both = oown[m, rows] + osib[m, rows].astype(jnp.float32)
            oown[m, rows] = both
            zsend[m, pl.ds(s * ZH, ZH)] = both.astype(jnp.bfloat16).reshape(ZH, 2, B, F)
        for i in range(Z // 2):
            q = s * (Z // 2) + rem(d + i, Z // 2)

            @pl.when(q != d)
            def _():
                za_copy(q).start()

    pair_sum(yl)
    h_arrival.wait_recv()
    down(1 - yl)
    pair_sum(1 - yl)

    for s in range(2):
        for m in range(YQ):
            @pl.when(is_owner(s, m))
            def _():
                yrb[yh] = zsend[m, :, s, :, F2:F]

            @pl.when(jnp.logical_not(is_owner(s, m)))
            def _():
                yb2_copy(s, m).start()

    y2t[:, span(x, N)] = ybuf[x].T

    mine = span(d, 2 * B)
    for k in near:
        q = depth_peer(k)
        za_arrival(q).wait_recv()
        for m in range(YQ):
            oown[m, mine, 0:F2] += zra[q, m].reshape(2 * B, F2).astype(jnp.float32)
    for m in range(YQ):
        ysa[m] = oown[m, mine, 0:F2].astype(jnp.bfloat16).reshape(2, B, F2)

    def ya_copy(s, m):
        return copy(
            ysa.at[m, s], yra.at[yh], yas.at[s * YQ + m], yar.at[yh], owner(s, m)
        )

    def ya_arrival(j):
        return copy(ysa.at[0, 0], yra.at[j], yas.at[0], yar.at[j], reader(j))

    for s in range(2):
        for m in range(YQ):
            @pl.when(is_owner(s, m))
            def _():
                yra[yh] = ysa[m, s]

            @pl.when(jnp.logical_not(is_owner(s, m)))
            def _():
                ya_copy(s, m).start()

    upper = jnp.zeros((Z, B, F2), jnp.float32)
    for j in range(YH):
        @pl.when(jnp.logical_not(home & (yh == j)))
        def _():
            yb2_arrival(j).wait_recv()
        upper = upper + yrb[j].astype(jnp.float32)
    zsb[...] = upper.astype(jnp.bfloat16)

    def zb2_copy(q):
        return copy(zsb.at[q], zrb.at[d], zbs.at[q], zbr.at[d], depth_device(q))

    def zb2_arrival(q):
        return copy(zsb.at[q], zrb.at[q], zbs.at[q], zbr.at[q], depth_device(q))

    for k in reversed(near):
        zb2_copy(depth_peer(k)).start()

    for k in range(1, XN):
        y2_arrival(k).wait_recv()
        yb_copy(k).start()

    output = x_ref[:, 0:F2].astype(jnp.float32)
    for j in range(YH):
        @pl.when(jnp.logical_not(home & (yh == j)))
        def _():
            ya_arrival(j).wait_recv()
        output = output + yra[j].astype(jnp.float32)
    outblk[:, 0:F2] = output.astype(jnp.bfloat16)
    output = x_ref[:, F2:F].astype(jnp.float32) + zsb[d].astype(jnp.float32)
    for k in near:
        q = depth_peer(k)
        zb2_arrival(q).wait_recv()
        output = output + zrb[q].astype(jnp.float32)
    outblk[:, F2:F] = output.astype(jnp.bfloat16)

    ga = Gather(outblk, obuf, ozb, a1, a2, a3, a4, a5, a6, a7, a8, a9, a10, a11, a12)
    ga.start()

    for k in range(1, XN):
        q = x_peer(XN - k)
        yb_arrival(k).wait_recv()
        y2t[:, span(q, N)] = y2buf[q].T

    ga.spread()

    def coef_of(q):
        s = seat(q)
        first = rem(q, XN)
        parity = lax.div(q, jnp.int32(XN))
        sums = st1recv[first] + st1recv[first + XN]
        lanes = jnp.where(parity == 0, sums[0:1, :], sums[1:2, :])
        inv = to_column(lax.rsqrt(lanes / features + norm_eps))
        both = gubuf[s].astype(jnp.float32)
        gate, up = both[:, 0:H], both[:, H:2 * H]
        sig = jax.nn.sigmoid(gate)
        coef[s, :, 0:H] = inv * (up * sig * (1.0 + gate * (1.0 - sig)))
        swish = gate * sig
        coef[s, :, H:2 * H] = inv * swish
        ht[:, span(s, L)] = (swish * up).astype(jnp.bfloat16).T

    for k in range(1, R):
        q = row_peer(k)

        @pl.when(q != pair_row)
        def _():
            q1_arrival(q).wait_recv()

    def coef_step(k):
        q = row_peer(k)
        gu_arrival(q).wait_recv()
        coef_of(q)

    loop(R, coef_step, 1)
    coef_of(r)

    ga.pass_on(near)
    ga.pass_on_upper()

    target = tgsend[...]
    for k in range(1, Z):
        t2_arrival(k).wait_recv()
        target = target + tg2[depth_peer(Z - k)]

    def stats(which, m):
        wide = obuf[which, m].reshape(N, F).astype(jnp.float32)
        head = gvbuf[which, m, 1:2, :]
        squares = jnp.sum(wide * wide, axis=1, keepdims=True)
        products = jnp.sum(wide * head, axis=1, keepdims=True)
        for s in range(2):
            part = slice(s * L, (s + 1) * L)
            st2send[s:s + 1, :] += to_lanes(squares[part])
            st2send[2 + s:3 + s, :] += to_lanes(products[part])

    st2send[...] = jnp.zeros_like(st2send)
    loop(YQ, lambda m: stats(core, m))
    ga.arrived()
    loop(YQ, lambda m: stats(1 - core, m))
    q2_copy = copy(st2send, st2recv, q2s, q2r, ypair)
    q2_copy.start()

    def o2_copy(k):
        q = x_peer(k)
        part = obuf.at[rem(q, 2), lax.div(q, jnp.int32(2)), pl.ds(core * ZH, ZH)]
        return copy(
            part, o2buf.at[x, pl.ds(core * ZH, ZH)], o2s.at[k], o2r.at[k], x_device(q)
        )

    def o2_arrival(k):
        q = x_peer(XN - k)
        part = o2buf.at[q, pl.ds(core * ZH, ZH)]
        return copy(part, part, o2s.at[k], o2r.at[k], x_device(q))

    def o3_copy(k):
        part = o2buf.at[x_peer(XN - k), pl.ds(core * ZH, ZH)]
        return copy(part, part, o3s.at[k], o3r.at[k], sibling)

    def o3_arrival(k):
        part = o2buf.at[x_peer(XN - k), pl.ds((1 - core) * ZH, ZH)]
        return copy(part, part, o3s.at[k], o3r.at[k], sibling)

    for k in range(1, XN):
        o2_copy(k).start()
    q2_copy.wait_recv()
    sums = st2send[...] + st2recv[...]
    inv_final = lax.rsqrt(sums[0:2] / features + norm_eps)
    values = sums[2:4] * inv_final
    val_ref[...] = jnp.broadcast_to(values[None], (4, 2, L)).reshape(8, L)
    slope = jnp.clip(values - target[0:2], -huber_delta, huber_delta)
    scale_lanes = inv_final * slope
    shrink_lanes = inv_final * inv_final * (slope * values / features)
    scsend[...] = jnp.concatenate([scale_lanes, shrink_lanes] * 2, axis=0)

    def sc_copy(k):
        return copy(scsend, screcv.at[x], scs.at[k], scr.at[k], x_device(x_peer(k)))

    def sc_arrival(k):
        q = x_peer(XN - k)
        return copy(scsend, screcv.at[q], scs.at[k], scr.at[k], x_device(q))

    for k in range(1, XN):
        sc_copy(k).start()

    def columns(lanes):
        return (
            jnp.concatenate([to_column(lanes[0:1]), to_column(lanes[1:2])], axis=0),
            jnp.concatenate([to_column(lanes[2:3]), to_column(lanes[3:4])], axis=0),
        )

    scale, shrink = columns(scsend[...])

    gsum[...] = jnp.zeros_like(gsum)
    ghpart[...] = jnp.zeros_like(ghpart)

    def grad_output(fl):
        which = rem(fl, 2)
        m = lax.div(fl, jnp.int32(2))
        wide = obuf[which, m].reshape(N, F).astype(jnp.float32)
        head = gvbuf[which, m, 1:2, :]
        gobuf[fl] = (scale * head - shrink * wide).astype(jnp.bfloat16)
        gsum[pl.ds(fl, 1), :] = jnp.sum(wide * scale, axis=0, keepdims=True)
        ghpart[...] += dot_t(gobuf[fl], wdbuf[fl])

    loop(XN, grad_output)

    g1_copy = copy(ghsend, ghrecv, g1s, g1r, ypair)
    ghsend[...] = ghpart[span(1 - yl, L)].astype(jnp.bfloat16)
    g1_copy.start()

    def gvo_copy(q):
        return copy(gsum, grecv.at[r], gvos.at[q], gvor.at[r], row_device(q))

    def gvo_arrival(q):
        return copy(gsum, grecv.at[q], gvos.at[q], gvor.at[q], row_device(q))

    def gh_copy(q):
        part = ghbuf.at[my_seat]
        return copy(part, part, ghs.at[q], ghr.at[r], row_device(q))

    def gh_arrival(q):
        part = ghbuf.at[seat(q)]
        return copy(part, part, ghs.at[q], ghr.at[q], row_device(q))

    g1_copy.wait_recv()
    ghbuf[my_seat] = (
        ghpart[span(yl, L)] + ghrecv[...].astype(jnp.float32)
    ).astype(jnp.bfloat16)
    for k in range(1, R):
        gh_copy(row_peer(k)).start()
    for k in range(1, R):
        gvo_copy(row_peer(k)).start()
    grecv[r] = gsum[...]

    go2buf[x] = gobuf[x]
    for k in range(1, XN):
        o2_arrival(k).wait_recv()
        o3_copy(k).start()
    head = gvbuf[rem(x, 2), lax.div(x, jnp.int32(2)), 1:2, :]
    for k in range(1, XN):
        q = x_peer(XN - k)
        sc_arrival(k).wait_recv()
        o3_arrival(k).wait_recv()
        scale, shrink = columns(screcv[q])
        wide = o2buf[q].reshape(N, F).astype(jnp.float32)
        go2buf[q] = (scale * head - shrink * wide).astype(jnp.bfloat16)
    tokens = XN * N
    tile = min(128, H)

    def down_weight_step(i):
        rows = span(i, tile)
        dd_ref[rows, :] = dot(ht[rows, :], go2buf[...].reshape(tokens, F)).astype(jnp.bfloat16)

    loop(H // tile, down_weight_step)

    def gg_of(s):
        grad = ghbuf[s].astype(jnp.float32)
        ggbuf[s, :, 0:H] = (grad * coef[s, :, 0:H]).astype(jnp.bfloat16)
        ggbuf[s, :, H:2 * H] = (grad * coef[s, :, H:2 * H]).astype(jnp.bfloat16)

    gg_of(my_seat)

    def gg_step(k):
        q = row_peer(k)
        gh_arrival(q).wait_recv()
        gg_of(seat(q))

    loop(R, gg_step, 1)

    tile_f = min(128, F)

    def weight_step(i):
        rows = span(i, tile_f)
        both = dot(y2t[rows, :], ggbuf[...].reshape(tokens, 2 * H)).astype(jnp.bfloat16)
        dg_ref[rows, :] = both[:, 0:H]
        du_ref[rows, :] = both[:, H:2 * H]

    loop(F // tile_f, weight_step)

    for k in range(1, R):
        gvo_arrival(row_peer(k)).wait_recv()
    head_sum = grecv[side * XN]
    for k in range(1, XN):
        head_sum = head_sum + grecv[side * XN + k]
    pick = lax.broadcasted_iota(jnp.int32, head_sum.shape, 0) == c - side * XN
    gval_ref[...] = jnp.broadcast_to(
        jnp.sum(jnp.where(pick, head_sum, 0.0), axis=0, keepdims=True), gval_ref.shape
    )

    gx.drain()
    ga.drain()
    for j in range(YH):
        @pl.when((yl == 0) & jnp.logical_not(home & (yh == j)))
        def _():
            gv_copy(j).wait_send()
    gb_copy.wait_send()
    t1_copy.wait_send()
    rs_copy.wait_send()
    q2_copy.wait_send()
    g1_copy.wait_send()

    w_drain(gate_w, up_w, down_w)
    h_copy.wait_send()

    def x_sends(k):
        y2_copy(k).wait_send()
        yb_copy(k).wait_send()
        o2_copy(k).wait_send()
        o3_copy(k).wait_send()
        sc_copy(k).wait_send()

    loop(XN, x_sends, 1)

    def row_sends(k):
        q = row_peer(k)
        q1_copy(q).wait_send()
        gu_copy(q).wait_send()
        gh_copy(q).wait_send()
        gvo_copy(q).wait_send()

    loop(R, row_sends, 1)

    def depth_sends(k):
        t2_copy(k).wait_send()
        za_copy(depth_peer(k)).wait_send()
        zb2_copy(depth_peer(k)).wait_send()

    loop(Z, depth_sends, 1)
    for s in range(2):
        ob_copy(s).wait_send()
        for m in range(YQ):
            @pl.when(jnp.logical_not(is_owner(s, m)))
            def _():
                ya_copy(s, m).wait_send()
                yb2_copy(s, m).wait_send()


def build(mesh):
    R, C, Z = mesh.shape["row"], mesh.shape["col"], mesh.shape["depth"]
    YH, XN = C // 2, R // 2
    YQ = YH // 2

    def per_device(residual, pre_gain, w_gate, w_up, w_down, value_head, sample_index, return_table):
        B, F = residual.shape
        H = w_gate.shape[1]
        N = Z * 2 * B
        L = N // 2
        r = lax.axis_index("row")
        d = lax.axis_index("depth")
        place = d * (2 * B) + (r // XN) * B
        target = jnp.take(return_table, sample_index)
        tile = lax.dynamic_update_slice(
            jnp.zeros((8, L), jnp.float32), target[None, :], (place // L, place % L)
        )
        gv = jnp.zeros((8, F), jnp.float32).at[0].set(pre_gain).at[1].set(value_head)

        bf, f32 = jnp.bfloat16, jnp.float32
        V = pltpu.VMEM
        dma = lambda *shape: pltpu.SemaphoreType.DMA(shape)
        F2 = F // 2
        gather = [
            dma(YH), dma(2 * YQ), dma(Z), dma(Z), dma(Z), dma(Z),
            dma(Z), dma(Z), dma(YH), dma(2 * YQ), dma(2 * YQ), dma(2 * YQ),
        ]
        scratch = [
            V((2, YQ, Z, 2, B, F), bf), V((Z, B, F2), bf),
            V((XN, N, F), bf), V((XN, N, F), bf), V((F, XN * N), bf),
            V((XN, F, H), bf), V((XN, F, H), bf), V((XN, H, F), bf),
            V((2, YQ, 8, F), f32), V((8, L), f32), V((8, L), f32), V((Z, 8, L), f32),
            V((N, 2 * H), f32), V((L, 2 * H), bf), V((L, 2 * H), bf),
            V((8, L), f32), V((R, 8, L), f32),
            V((2, L, H), bf), V((H, R * L), bf), V((R, L, 2 * H), bf), V((R, L, 2 * H), f32),
            V((YQ, N, F), bf), V((YQ, N, F), bf), V((YQ, N, F), f32),
            V((YQ, Z, 2, B, F), bf), V((Z, YQ, 2, B, F2), bf), V((YH, B, F2), bf),
            V((YH, Z, B, F2), bf), V((Z, B, F2), bf), V((YQ, 2, B, F2), bf), V((Z, B, F2), bf),
            V((B, F), bf), V((2, YQ, Z, 2, B, F), bf), V((Z, B, F2), bf),
            V((8, L), f32), V((8, L), f32), V((8, L), f32), V((XN, 8, L), f32),
            V((XN, Z, 2, B, F), bf), V((XN, N, F), bf), V((XN, N, F), bf),
            V((N, H), f32), V((L, H), bf), V((L, H), bf),
            V((R, L, H), bf), V((R, L, 2 * H), bf), V((8, F), f32), V((R, 8, F), f32),
            *gather,
            dma(YH), dma(YQ), dma(), dma(), dma(), dma(), dma(Z), dma(Z),
            dma(3), dma(4), dma(4), dma(4), dma(4), dma(4), dma(4),
            dma(R), dma(R), dma(), dma(), dma(XN), dma(XN), dma(XN), dma(XN),
            dma(), dma(), dma(R), dma(R),
            dma(2), dma(2), dma(Z), dma(Z), dma(2 * YQ), dma(YH), dma(2 * YQ), dma(YH),
            dma(Z), dma(Z),
            *gather,
            dma(), dma(), dma(XN), dma(XN), dma(XN), dma(XN), dma(XN), dma(XN),
            dma(), dma(), dma(R), dma(R), dma(R), dma(R),
        ]
        vmem = pl.BlockSpec(memory_space=pltpu.VMEM)
        hbm = pl.BlockSpec(memory_space=pl.ANY)
        dg, du, dd, values, gval = pl.pallas_call(
            functools.partial(kernel, R, YH, Z, B, F, H),
            out_shape=(
                jax.ShapeDtypeStruct((F, H), bf),
                jax.ShapeDtypeStruct((F, H), bf),
                jax.ShapeDtypeStruct((H, F), bf),
                jax.ShapeDtypeStruct((8, L), f32),
                jax.ShapeDtypeStruct((8, F), f32),
            ),
            in_specs=[vmem, vmem, vmem, hbm, hbm, hbm],
            out_specs=(vmem,) * 5,
            scratch_shapes=scratch,
            compiler_params=pltpu.CompilerParams(
                collective_id=0, has_side_effects=True, vmem_limit_bytes=40 * 1024 * 1024
            ),
        )(residual, gv, tile, w_gate, w_up, w_down)
        values = lax.dynamic_slice(values, (place // L, place % L), (1, B))[0]
        return values, dg, du, dd, gval[0]

    return per_device


def solution(mesh):
    placed = (
        P(("row", "depth"), "col"),
        P("col"),
        P("row", ("col", "depth")),
        P("row", ("col", "depth")),
        P(("col", "depth"), "row"),
        P("col"),
        P(("row", "depth")),
        P(),
    )
    return jax.shard_map(
        build(mesh),
        mesh=mesh,
        in_specs=placed,
        out_specs=(
            P(("row", "depth")),
            P("row", ("col", "depth")),
            P("row", ("col", "depth")),
            P(("col", "depth"), "row"),
            P("col"),
        ),
        check_vma=False,
    )
```

```python
import functools

import jax
import jax.numpy as jnp
from jax import lax
from jax.experimental import pallas as pl
from jax.experimental.pallas import tpu as pltpu
from jax.sharding import PartitionSpec as P

MESH = pl.DeviceIdType.MESH
norm_eps = 1e-06
huber_delta = 1.0
VMEM_MB = 56


def rem(value, size):
    return lax.rem(value, jnp.int32(size))


def dot(left, right):
    return jnp.dot(left, right, preferred_element_type=jnp.float32)


def dot_t(left, right):
    return lax.dot_general(
        left, right, (((1,), (1,)), ((), ())), preferred_element_type=jnp.float32
    )


def kernel(
    R, YH, Z, B, F, H,
    x_ref, gain_ref, head_ref, index_ref, table_ref, wg_ref, wu_ref, wd_ref,
    dg_ref, du_ref, dd_ref, val_ref, gval_ref,
    xbuf, xzb, ybuf, y2buf, y2t, wgbuf, wubuf, wdbuf, gnbuf, hdbuf, xblk, index, table,
    tgown, tg1, tgsend, tg2,
    acc, stat, rssend, rsrecv, st1send, st1recv, hbuf, ht, gubuf, coef,
    osend, osib, oown, zsend, zra, yra, yrb, zrb, ysa, zsb, outblk, obuf, ozb,
    st2send, st2recv, scsend, screcv, o2buf, gobuf, go2buf,
    ghpart, ghsend, ghrecv, ghbuf, ggbuf, gsum, grecv,
    x1, x2, x3, x4, x5, x6, x7, x8, x9, x10, x11, x12, gvs, gvr, hds, hdr, gbs, gbr, los, t1s, t1r, t2s, t2r,
    wls, wgs, wgr, wus, wur, wds, wdr, q1s, q1r, rss, rsr, y2s, y2r, ybs, ybr, hs, hr, gps, gpr, gus, gur,
    obs, obr, zas, zar, yas, yar, ybbs, ybbr, zbs, zbr,
    a1, a2, a3, a4, a5, a6, a7, a8, a9, a10, a11, a12, q2s, q2r, scs, scr,
    o2s, o2r, o3s, o3r, g1s, g1r, ghs, ghr, gvos, gvor,
):
    XN, YQ = R // 2, YH // 2
    N = Z * 2 * B
    L = N // 2
    features = R * F
    F2 = F // 2
    ZH = Z // 2
    lo, hi = pl.ds(0, F2), pl.ds(F2, F2)
    r = lax.axis_index("row")
    c = lax.axis_index("col")
    d = lax.axis_index("depth")
    x = rem(r, XN)
    yl = lax.div(r, jnp.int32(XN))
    core = rem(c, 2)
    yh = lax.div(c, jnp.int32(2))
    side = lax.div(yh, jnp.int32(YQ))
    mloc = rem(yh, YQ)
    home = yl == side
    sibling = (r, 2 * yh + 1 - core, d)
    ypair = ((1 - yl) * XN + x, c, d)

    def copy(src, dst, send, recv, device):
        return pltpu.make_async_remote_copy(
            src_ref=src, dst_ref=dst, send_sem=send, recv_sem=recv,
            device_id=device, device_id_type=MESH,
        )

    def row_peer(k):
        return rem(r + k, R)

    def depth_peer(k):
        return rem(d + k, Z)

    def x_peer(k):
        return rem(x + k, XN)

    def row_device(q):
        return (q, c, d)

    def depth_device(q):
        return (r, c, q)

    def x_device(q):
        return (yl * XN + q, c, d)

    def seat(q):
        return rem(q, XN) * 2 + lax.div(q, jnp.int32(XN))

    my_seat = x * 2 + yl

    def reader(j):
        return (side * XN + x, 2 * j + core, d)

    def owner(s, m):
        return (s * XN + x, 2 * (yl * YQ + m) + core, d)

    def is_owner(s, m):
        return (yl == s) & (yh == yl * YQ + m)

    def span(index, size):
        return pl.ds(pl.multiple_of(index * size, size), size)

    def loop(count, body, start=0):
        def step(k, carry):
            body(k)
            return carry
        lax.fori_loop(start, count, step, 0)

    eye = (
        lax.broadcasted_iota(jnp.int32, (L, L), 0)
        == lax.broadcasted_iota(jnp.int32, (L, L), 1)
    )

    def to_lanes(column):
        return jnp.sum(jnp.where(eye, column, 0.0), axis=0, keepdims=True)

    def to_column(lanes):
        return jnp.sum(jnp.where(eye, lanes, 0.0), axis=1, keepdims=True)

    local_x = pltpu.make_async_copy(x_ref, xblk, los.at[0])
    local_index = pltpu.make_async_copy(index_ref, index, los.at[1])
    local_table = pltpu.make_async_copy(table_ref, table, los.at[2])
    for one in (local_x, local_index, local_table):
        one.start()

    barrier = pltpu.get_barrier_semaphore()

    def greet(device):
        pl.semaphore_signal(barrier, inc=1, device_id=device, device_id_type=MESH)

    for k in range(1, R):
        greet(row_device(row_peer(k)))
    for k in range(1, Z):
        greet(depth_device(depth_peer(k)))
    greet(sibling)
    for j in range(YH):
        @pl.when(jnp.logical_not(home & (yh == j)))
        def _():
            greet(reader(j))
    for s in range(2):
        for m in range(YQ):
            @pl.when(jnp.logical_not(is_owner(s, m)))
            def _():
                greet(owner(s, m))
    pl.semaphore_wait(
        barrier, (R - 1) + (Z - 1) + 1 + YH + 2 * YQ - jnp.where(home, 2, 0)
    )

    near = []
    for k in range(1, Z // 2 + 1):
        near.append(k)
        if Z - k > k:
            near.append(Z - k)

    class Gather:
        def __init__(self, src, local, buf, zb, *sems):
            self.src, self.local, self.buf, self.zb = src, local, buf, zb
            (self.ays, self.ayr, self.azs, self.azr, self.ass, self.asr,
             self.bzs, self.bzr, self.bys, self.byr, self.bss, self.bsr) = sems

        def ay_copy(self, j):
            return copy(
                self.src.at[:, lo], self.buf.at[core, mloc, d, yl, :, lo],
                self.ays.at[j], self.ayr.at[yl * YQ + mloc], reader(j),
            )

        def ay_arrival(self, s, m):
            return copy(
                self.src.at[:, lo], self.buf.at[core, m, d, s, :, lo],
                self.ays.at[0], self.ayr.at[s * YQ + m], owner(s, m),
            )

        def az_copy(self, k):
            part = self.buf.at[core, :, d, :, :, lo]
            return copy(
                part, part, self.azs.at[k], self.azr.at[k], depth_device(depth_peer(k))
            )

        def az_arrival(self, k):
            q = depth_peer(Z - k)
            part = self.buf.at[core, :, q, :, :, lo]
            return copy(part, part, self.azs.at[k], self.azr.at[k], depth_device(q))

        def as_copy(self, k):
            part = self.buf.at[core, :, depth_peer(Z - k), :, :, lo]
            return copy(part, part, self.ass.at[k], self.asr.at[k], sibling)

        def as_arrival(self, k):
            part = self.buf.at[1 - core, :, depth_peer(Z - k), :, :, lo]
            return copy(part, part, self.ass.at[k], self.asr.at[k], sibling)

        def bz_copy(self, k):
            return copy(
                self.src.at[:, hi], self.zb.at[d], self.bzs.at[k], self.bzr.at[k],
                depth_device(depth_peer(k)),
            )

        def bz_arrival(self, k):
            q = depth_peer(Z - k)
            return copy(
                self.src.at[:, hi], self.zb.at[q], self.bzs.at[k], self.bzr.at[k],
                depth_device(q),
            )

        def by_copy(self, j):
            return copy(
                self.zb, self.buf.at[core, mloc, :, yl, :, hi],
                self.bys.at[j], self.byr.at[yl * YQ + mloc], reader(j),
            )

        def by_arrival(self, s, m):
            return copy(
                self.zb, self.buf.at[core, m, :, s, :, hi],
                self.bys.at[0], self.byr.at[s * YQ + m], owner(s, m),
            )

        def bs_copy(self, s, m):
            part = self.buf.at[core, m, :, s, :, hi]
            i = s * YQ + m
            return copy(part, part, self.bss.at[i], self.bsr.at[i], sibling)

        def bs_arrival(self, s, m):
            part = self.buf.at[1 - core, m, :, s, :, hi]
            i = s * YQ + m
            return copy(part, part, self.bss.at[i], self.bsr.at[i], sibling)

        def start(self):
            for j in range(YH):
                @pl.when(jnp.logical_not(home & (yh == j)))
                def _():
                    self.ay_copy(j).start()
            for k in reversed(near):
                self.bz_copy(k).start()

        def keep(self):
            @pl.when(home)
            def _():
                self.buf[core, mloc, d, yl, :, 0:F2] = self.local[:, 0:F2]
            self.zb[d] = self.local[:, F2:F]

        def spread(self):
            for s in range(2):
                for m in range(YQ):
                    @pl.when(jnp.logical_not(is_owner(s, m)))
                    def _():
                        self.ay_arrival(s, m).wait_recv()
            for k in reversed(near):
                self.az_copy(k).start()
            self.as_copy(0).start()
            for k in near:
                self.bz_arrival(k).wait_recv()
            for j in range(YH):
                @pl.when(home & (yh == j))
                def _():
                    self.buf[core, mloc, :, yl, :, F2:F] = self.zb[...]

                @pl.when(jnp.logical_not(home & (yh == j)))
                def _():
                    self.by_copy(j).start()

        def pass_on(self, ks):
            for k in ks:
                self.az_arrival(k).wait_recv()
                self.as_copy(k).start()

        def pass_on_upper(self):
            for s in range(2):
                for m in range(YQ):
                    @pl.when(jnp.logical_not(is_owner(s, m)))
                    def _():
                        self.by_arrival(s, m).wait_recv()
                    self.bs_copy(s, m).start()

        def arrived(self):
            for k in [0] + near:
                self.as_arrival(k).wait_recv()
            for s in range(2):
                for m in range(YQ):
                    self.bs_arrival(s, m).wait_recv()

        def drain(self):
            for j in range(YH):
                @pl.when(jnp.logical_not(home & (yh == j)))
                def _():
                    self.ay_copy(j).wait_send()
                    self.by_copy(j).wait_send()
            for k in range(1, Z):
                self.az_copy(k).wait_send()
                self.bz_copy(k).wait_send()
            for k in range(Z):
                self.as_copy(k).wait_send()
            for s in range(2):
                for m in range(YQ):
                    self.bs_copy(s, m).wait_send()

    gx = Gather(x_ref, xblk, xbuf, xzb, x1, x2, x3, x4, x5, x6, x7, x8, x9, x10, x11, x12)
    gx.start()

    def gn_copy(j):
        return copy(gain_ref, gnbuf.at[core, mloc], gvs.at[j], gvr.at[mloc], reader(j))

    def hd_copy(j):
        return copy(head_ref, hdbuf.at[core, mloc], hds.at[j], hdr.at[mloc], reader(j))

    def gn_arrival(m):
        return copy(gain_ref, gnbuf.at[core, m], gvs.at[0], gvr.at[m], owner(0, m))

    def hd_arrival(m):
        return copy(head_ref, hdbuf.at[core, m], hds.at[0], hdr.at[m], owner(0, m))

    gn_local = pltpu.make_async_copy(gain_ref, gnbuf.at[core, mloc], los.at[3])
    hd_local = pltpu.make_async_copy(head_ref, hdbuf.at[core, mloc], los.at[4])

    @pl.when((yl == 0) & home)
    def _():
        gn_local.start()
        hd_local.start()

    for j in range(YH):
        @pl.when((yl == 0) & jnp.logical_not(home & (yh == j)))
        def _():
            gn_copy(j).start()
            hd_copy(j).start()

    def local_weights():
        return (
            pltpu.make_async_copy(wg_ref, wgbuf.at[x], wls.at[0]),
            pltpu.make_async_copy(wu_ref, wubuf.at[x], wls.at[1]),
            pltpu.make_async_copy(wd_ref, wdbuf.at[x], wls.at[2]),
        )

    for one in local_weights():
        one.start()

    def w_copy(ref, buf, send, recv, k):
        return copy(ref, buf.at[x], send.at[k], recv.at[k], x_device(x_peer(k)))

    def w_arrival(ref, buf, send, recv, k):
        q = x_peer(XN - k)
        return copy(ref, buf.at[q], send.at[k], recv.at[k], x_device(q))

    def w_onward(ref, buf, send, recv, k):
        rows = ref.shape[0] // 2
        part = buf.at[x_peer(XN - k), pl.ds(0 if k == 1 else rows, rows)]
        return copy(part, part, send.at[k - 1], recv.at[k - 1], x_device(x_peer(k)))

    def w_onward_arrival(ref, buf, send, recv, k):
        rows = ref.shape[0] // 2
        part = buf.at[x_peer(2), pl.ds(0 if k == 1 else rows, rows)]
        return copy(part, part, send.at[k - 1], recv.at[k - 1], x_device(x_peer(XN - k)))

    gate_w = (wg_ref, wgbuf, wgs, wgr)
    up_w = (wu_ref, wubuf, wus, wur)
    down_w = (wd_ref, wdbuf, wds, wdr)
    sides = (1,) if XN == 2 else (1, 3)

    def w_start(*which):
        for k in sides:
            for w in which:
                w_copy(*w, k).start()

    def w_turn(*which):
        for k in sides:
            for w in which:
                w_arrival(*w, k).wait_recv()
                if XN == 4:
                    w_onward(*w, k).start()

    def w_finish(*which):
        if XN == 4:
            for k in sides:
                for w in which:
                    w_onward_arrival(*w, k).wait_recv()

    def w_drain(*which):
        for k in sides:
            for w in which:
                w_copy(*w, k).wait_send()
                if XN == 4:
                    w_onward(*w, k).wait_send()

    w_start(gate_w, up_w)

    local_x.wait()
    gx.keep()

    local_index.wait()
    local_table.wait()
    place = d * (2 * B) + yl * B
    place_row = lax.div(place, jnp.int32(L))
    place_lane = rem(place, L)
    table_lanes = lax.broadcasted_iota(jnp.int32, (1, 128), 1)
    lanes = lax.broadcasted_iota(jnp.int32, (1, L), 1)

    def look_up(i, found):
        entry = index[0, i]
        line = table[pl.ds(lax.div(entry, jnp.int32(128)), 1), :]
        value = jnp.sum(
            jnp.where(table_lanes == rem(entry, 128), line, 0.0), axis=1, keepdims=True
        )
        return found + jnp.where(lanes == place_lane + i, value, 0.0)

    found = lax.fori_loop(0, B, look_up, jnp.zeros((1, L), jnp.float32))
    tile_rows = lax.broadcasted_iota(jnp.int32, (8, L), 0)
    tgown[...] = jnp.where(tile_rows == place_row, found, 0.0)
    t1_copy = copy(tgown, tg1, t1s, t1r, ypair)
    t1_copy.start()

    gx.spread()

    for m in range(YQ):
        here = (yl == 0) & is_owner(0, m)

        @pl.when(here)
        def _():
            gn_local.wait()
            hd_local.wait()

        @pl.when(jnp.logical_not(here))
        def _():
            gn_arrival(m).wait_recv()
            hd_arrival(m).wait_recv()
    gb_copy = copy(gnbuf.at[core], gnbuf.at[core], gbs.at[0], gbr.at[0], sibling)
    hb_copy = copy(hdbuf.at[core], hdbuf.at[core], gbs.at[1], gbr.at[1], sibling)
    gb_arrival = copy(gnbuf.at[1 - core], gnbuf.at[1 - core], gbs.at[0], gbr.at[0], sibling)
    hb_arrival = copy(hdbuf.at[1 - core], hdbuf.at[1 - core], gbs.at[1], gbr.at[1], sibling)
    gb_copy.start()
    hb_copy.start()

    t1_copy.wait_recv()
    tgsend[...] = tgown[...] + tg1[...]

    def t2_copy(k):
        return copy(tgsend, tg2.at[d], t2s.at[k], t2r.at[k], depth_device(depth_peer(k)))

    def t2_arrival(k):
        q = depth_peer(Z - k)
        return copy(tgsend, tg2.at[q], t2s.at[k], t2r.at[k], depth_device(q))

    for k in range(1, Z):
        t2_copy(k).start()

    w_turn(gate_w, up_w)
    w_start(down_w)
    gx.pass_on(near)
    gx.pass_on_upper()
    for one in local_weights():
        one.wait()

    def fold(wide):
        total = wide[:, 0:128]
        for i in range(1, F // 128):
            total = total + wide[:, 128 * i:128 * (i + 1)]
        return total

    def lane_sums(folded):
        column = jnp.sum(folded, axis=1, keepdims=True)
        return [to_lanes(column[s * L:(s + 1) * L]) for s in range(2)]

    def gate_up(which, m):
        fl = 2 * m + which
        wide = xbuf[which, m].reshape(N, F).astype(jnp.float32)
        scaled = (wide * gnbuf[which, m]).astype(jnp.bfloat16)
        ybuf[fl] = scaled
        acc[:, 0:H] += dot(scaled, wgbuf[fl])
        acc[:, H:2 * H] += dot(scaled, wubuf[fl])
        stat[0] += fold(wide * wide)

    acc[...] = jnp.zeros_like(acc)
    stat[...] = jnp.zeros_like(stat)
    w_finish(gate_w, up_w)
    loop(YQ, lambda m: gate_up(core, m))
    w_turn(down_w)
    gb_arrival.wait_recv()
    gx.arrived()
    loop(YQ, lambda m: gate_up(1 - core, m))

    rs_copy = copy(rssend, rsrecv, rss, rsr, ypair)
    rssend[...] = acc[span(1 - yl, L)].astype(jnp.bfloat16)

    def q1_copy(q):
        return copy(st1send, st1recv.at[r], q1s.at[q], q1r.at[r], row_device(q))

    def q1_arrival(q):
        return copy(st1send, st1recv.at[q], q1s.at[q], q1r.at[q], row_device(q))

    pair_row = (1 - yl) * XN + x
    st1send[...] = jnp.concatenate(lane_sums(stat[0]) * 4, axis=0)
    q1_copy(pair_row).start()
    rs_copy.start()
    for k in range(1, R):
        q = row_peer(k)

        @pl.when(q != pair_row)
        def _():
            q1_copy(q).start()
    st1recv[r] = st1send[...]

    near_half = span(core, L)
    far_half = span(1 - core, L)

    def y2_copy(k):
        q = x_peer(k)
        return copy(
            ybuf.at[q, near_half], y2buf.at[x, near_half], y2s.at[k], y2r.at[k], x_device(q)
        )

    def y2_arrival(k):
        q = x_peer(XN - k)
        part = y2buf.at[q, near_half]
        return copy(part, part, y2s.at[k], y2r.at[k], x_device(q))

    def yb_copy(k):
        part = y2buf.at[x_peer(XN - k), near_half]
        return copy(part, part, ybs.at[k], ybr.at[k], sibling)

    def yb_arrival(k):
        part = y2buf.at[x_peer(XN - k), far_half]
        return copy(part, part, ybs.at[k], ybr.at[k], sibling)

    for k in range(1, XN):
        y2_copy(k).start()

    q1_arrival(pair_row).wait_recv()
    squares = st1send[...] + st1recv[pair_row]
    inv_lanes = lax.rsqrt(squares / features + norm_eps)
    inv_mine = jnp.where(yl == 0, inv_lanes[0:1, :], inv_lanes[1:2, :])
    inv_norm = to_column(inv_mine)
    rs_copy.wait_recv()
    total = (acc[span(yl, L)] + rsrecv[...].astype(jnp.float32)) * inv_norm
    gate, up = total[:, 0:H], total[:, H:2 * H]
    hbuf[yl] = (gate * jax.nn.sigmoid(gate) * up).astype(jnp.bfloat16)

    h_copy = copy(hbuf.at[yl], hbuf.at[yl], hs, hr, ypair)
    h_arrival = copy(hbuf.at[1 - yl], hbuf.at[1 - yl], hs, hr, ypair)

    gp_copy = copy(gubuf.at[my_seat], gubuf.at[my_seat], gps, gpr, ypair)
    pair_seat = x * 2 + 1 - yl
    gp_arrival = copy(gubuf.at[pair_seat], gubuf.at[pair_seat], gps, gpr, ypair)

    def gu_copy(k):
        part = gubuf.at[pl.ds(x * 2, 2)]
        return copy(part, part, gus.at[k], gur.at[k], x_device(x_peer(k)))

    def gu_arrival(k):
        q = x_peer(XN - k)
        part = gubuf.at[pl.ds(q * 2, 2)]
        return copy(part, part, gus.at[k], gur.at[k], x_device(q))

    h_copy.start()
    gubuf[my_seat] = total.astype(jnp.bfloat16)

    w_finish(down_w)

    def ob_copy(s):
        part = pl.ds(pl.multiple_of(s * L, L), L)
        return copy(osend.at[:, part], osib.at[:, part], obs.at[s], obr.at[s], sibling)

    def down(s):
        rows = span(s, L)
        act = hbuf[s]
        for m in range(YQ):
            osend[m, rows] = dot(act, wdbuf[2 * m + 1 - core]).astype(jnp.bfloat16)
        ob_copy(s).start()
        for m in range(YQ):
            oown[m, rows] = dot(act, wdbuf[2 * m + core])

    down(yl)
    gp_copy.start()

    def za_copy(q):
        return copy(
            zsend.at[:, q, :, :, lo], zra.at[d], zas.at[q], zar.at[d], depth_device(q)
        )

    def za_arrival(q):
        return copy(
            zsend.at[:, q, :, :, lo], zra.at[q], zas.at[q], zar.at[q], depth_device(q)
        )

    def yb2_copy(s, m):
        return copy(
            zsend.at[m, :, s, :, hi], yrb.at[yh], ybbs.at[s * YQ + m], ybbr.at[yh], owner(s, m)
        )

    def yb2_arrival(j):
        return copy(
            zsend.at[0, :, 0, :, hi], yrb.at[j], ybbs.at[0], ybbr.at[j], reader(j)
        )

    def pair_sum(s):
        rows = span(s, L)
        ob_copy(s).wait_recv()
        for m in range(YQ):
            both = oown[m, rows] + osib[m, rows].astype(jnp.float32)
            oown[m, rows] = both
            zsend[m, pl.ds(s * ZH, ZH)] = both.astype(jnp.bfloat16).reshape(ZH, 2, B, F)
        for i in range(Z // 2):
            q = s * (Z // 2) + rem(d + i, Z // 2)

            @pl.when(q != d)
            def _():
                za_copy(q).start()

    pair_sum(yl)
    h_arrival.wait_recv()
    down(1 - yl)
    pair_sum(1 - yl)
    gp_arrival.wait_recv()
    for k in range(1, XN):
        gu_copy(k).start()

    for s in range(2):
        for m in range(YQ):
            @pl.when(is_owner(s, m))
            def _():
                yrb[yh] = zsend[m, :, s, :, F2:F]

            @pl.when(jnp.logical_not(is_owner(s, m)))
            def _():
                yb2_copy(s, m).start()

    y2t[:, span(x, N)] = ybuf[x].T

    mine = span(d, 2 * B)
    for k in near:
        q = depth_peer(k)
        za_arrival(q).wait_recv()
        for m in range(YQ):
            oown[m, mine, 0:F2] += zra[q, m].reshape(2 * B, F2).astype(jnp.float32)
    for m in range(YQ):
        ysa[m] = oown[m, mine, 0:F2].astype(jnp.bfloat16).reshape(2, B, F2)

    def ya_copy(s, m):
        return copy(
            ysa.at[m, s], yra.at[yh], yas.at[s * YQ + m], yar.at[yh], owner(s, m)
        )

    def ya_arrival(j):
        return copy(ysa.at[0, 0], yra.at[j], yas.at[0], yar.at[j], reader(j))

    for s in range(2):
        for m in range(YQ):
            @pl.when(is_owner(s, m))
            def _():
                yra[yh] = ysa[m, s]

            @pl.when(jnp.logical_not(is_owner(s, m)))
            def _():
                ya_copy(s, m).start()

    upper = jnp.zeros((Z, B, F2), jnp.float32)
    for j in range(YH):
        @pl.when(jnp.logical_not(home & (yh == j)))
        def _():
            yb2_arrival(j).wait_recv()
        upper = upper + yrb[j].astype(jnp.float32)
    zsb[...] = upper.astype(jnp.bfloat16)

    def zb2_copy(q):
        return copy(zsb.at[q], zrb.at[d], zbs.at[q], zbr.at[d], depth_device(q))

    def zb2_arrival(q):
        return copy(zsb.at[q], zrb.at[q], zbs.at[q], zbr.at[q], depth_device(q))

    for k in reversed(near):
        zb2_copy(depth_peer(k)).start()

    for k in range(1, XN):
        y2_arrival(k).wait_recv()
        yb_copy(k).start()

    output = xblk[:, 0:F2].astype(jnp.float32)
    for j in range(YH):
        @pl.when(jnp.logical_not(home & (yh == j)))
        def _():
            ya_arrival(j).wait_recv()
        output = output + yra[j].astype(jnp.float32)
    outblk[:, 0:F2] = output.astype(jnp.bfloat16)
    output = xblk[:, F2:F].astype(jnp.float32) + zsb[d].astype(jnp.float32)
    for k in near:
        q = depth_peer(k)
        zb2_arrival(q).wait_recv()
        output = output + zrb[q].astype(jnp.float32)
    outblk[:, F2:F] = output.astype(jnp.bfloat16)

    ga = Gather(outblk, outblk, obuf, ozb, a1, a2, a3, a4, a5, a6, a7, a8, a9, a10, a11, a12)
    ga.start()
    ga.keep()

    for k in range(1, XN):
        q = x_peer(XN - k)
        yb_arrival(k).wait_recv()
        y2t[:, span(q, N)] = y2buf[q].T

    ga.spread()

    def coef_of(q):
        s = seat(q)
        first = rem(q, XN)
        parity = lax.div(q, jnp.int32(XN))
        sums = st1recv[first] + st1recv[first + XN]
        lanes = jnp.where(parity == 0, sums[0:1, :], sums[1:2, :])
        inv = to_column(lax.rsqrt(lanes / features + norm_eps))
        both = gubuf[s].astype(jnp.float32)
        gate, up = both[:, 0:H], both[:, H:2 * H]
        sig = jax.nn.sigmoid(gate)
        coef[s, :, 0:H] = inv * (up * sig * (1.0 + gate * (1.0 - sig)))
        swish = gate * sig
        coef[s, :, H:2 * H] = inv * swish
        ht[:, span(s, L)] = (swish * up).astype(jnp.bfloat16).T

    for k in range(1, R):
        q = row_peer(k)

        @pl.when(q != pair_row)
        def _():
            q1_arrival(q).wait_recv()

    coef_of(x)
    coef_of(XN + x)

    def coef_step(k):
        gu_arrival(k).wait_recv()
        q = x_peer(XN - k)
        coef_of(q)
        coef_of(XN + q)

    loop(XN, coef_step, 1)

    ga.pass_on(near)
    ga.pass_on_upper()

    target = tgsend[...]
    for k in range(1, Z):
        t2_arrival(k).wait_recv()
        target = target + tg2[depth_peer(Z - k)]

    def stats(which, m):
        wide = obuf[which, m].reshape(N, F).astype(jnp.float32)
        stat[0] += fold(wide * wide)
        stat[1] += fold(wide * hdbuf[which, m])

    stat[...] = jnp.zeros_like(stat)
    loop(YQ, lambda m: stats(core, m))
    hb_arrival.wait_recv()
    ga.arrived()
    loop(YQ, lambda m: stats(1 - core, m))
    st2send[...] = jnp.concatenate((lane_sums(stat[0]) + lane_sums(stat[1])) * 2, axis=0)
    q2_copy = copy(st2send, st2recv, q2s, q2r, ypair)
    q2_copy.start()

    def o2_copy(k):
        q = x_peer(k)
        part = obuf.at[rem(q, 2), lax.div(q, jnp.int32(2)), pl.ds(core * ZH, ZH)]
        return copy(
            part, o2buf.at[x, pl.ds(core * ZH, ZH)], o2s.at[k], o2r.at[k], x_device(q)
        )

    def o2_arrival(k):
        q = x_peer(XN - k)
        part = o2buf.at[q, pl.ds(core * ZH, ZH)]
        return copy(part, part, o2s.at[k], o2r.at[k], x_device(q))

    def o3_copy(k):
        part = o2buf.at[x_peer(XN - k), pl.ds(core * ZH, ZH)]
        return copy(part, part, o3s.at[k], o3r.at[k], sibling)

    def o3_arrival(k):
        part = o2buf.at[x_peer(XN - k), pl.ds((1 - core) * ZH, ZH)]
        return copy(part, part, o3s.at[k], o3r.at[k], sibling)

    for k in range(1, XN):
        o2_copy(k).start()
    q2_copy.wait_recv()
    sums = st2send[...] + st2recv[...]
    inv_final = lax.rsqrt(sums[0:2] / features + norm_eps)
    values = sums[2:4] * inv_final
    value_row = jnp.where(place_row == 0, values[0:1], values[1:2])
    own_values = jnp.sum(
        jnp.where(
            lax.broadcasted_iota(jnp.int32, (B, L), 1)
            == place_lane + lax.broadcasted_iota(jnp.int32, (B, L), 0),
            value_row, 0.0,
        ),
        axis=1, keepdims=True,
    )
    val_ref[...] = jnp.sum(
        jnp.where(
            lax.broadcasted_iota(jnp.int32, (B, 128), 1)
            == lax.broadcasted_iota(jnp.int32, (B, 128), 0),
            own_values, 0.0,
        ),
        axis=0, keepdims=True,
    )
    slope = jnp.clip(values - target[0:2], -huber_delta, huber_delta)
    scale_lanes = inv_final * slope
    shrink_lanes = inv_final * inv_final * (slope * values / features)
    scsend[...] = jnp.concatenate([scale_lanes, shrink_lanes] * 2, axis=0)

    def sc_copy(k):
        return copy(scsend, screcv.at[x], scs.at[k], scr.at[k], x_device(x_peer(k)))

    def sc_arrival(k):
        q = x_peer(XN - k)
        return copy(scsend, screcv.at[q], scs.at[k], scr.at[k], x_device(q))

    for k in range(1, XN):
        sc_copy(k).start()

    def columns(lanes):
        return (
            jnp.concatenate([to_column(lanes[0:1]), to_column(lanes[1:2])], axis=0),
            jnp.concatenate([to_column(lanes[2:3]), to_column(lanes[3:4])], axis=0),
        )

    scale, shrink = columns(scsend[...])

    gsum[...] = jnp.zeros_like(gsum)
    ghpart[...] = jnp.zeros_like(ghpart)

    def grad_output(fl):
        which = rem(fl, 2)
        m = lax.div(fl, jnp.int32(2))
        wide = obuf[which, m].reshape(N, F).astype(jnp.float32)
        head = hdbuf[which, m]
        gobuf[fl] = (scale * head - shrink * wide).astype(jnp.bfloat16)
        gsum[pl.ds(fl, 1), :] = jnp.sum(wide * scale, axis=0, keepdims=True)
        ghpart[...] += dot_t(gobuf[fl], wdbuf[fl])

    loop(XN, grad_output)

    g1_copy = copy(ghsend, ghrecv, g1s, g1r, ypair)
    ghsend[...] = ghpart[span(1 - yl, L)].astype(jnp.bfloat16)
    g1_copy.start()

    def gvo_copy(q):
        return copy(gsum, grecv.at[r], gvos.at[q], gvor.at[r], row_device(q))

    def gvo_arrival(q):
        return copy(gsum, grecv.at[q], gvos.at[q], gvor.at[q], row_device(q))

    def gh_copy(q):
        part = ghbuf.at[my_seat]
        return copy(part, part, ghs.at[q], ghr.at[r], row_device(q))

    def gh_arrival(q):
        part = ghbuf.at[seat(q)]
        return copy(part, part, ghs.at[q], ghr.at[q], row_device(q))

    g1_copy.wait_recv()
    ghbuf[my_seat] = (
        ghpart[span(yl, L)] + ghrecv[...].astype(jnp.float32)
    ).astype(jnp.bfloat16)
    for k in range(1, R):
        gh_copy(row_peer(k)).start()
    for k in range(1, R):
        gvo_copy(row_peer(k)).start()
    grecv[r] = gsum[...]

    go2buf[x] = gobuf[x]
    for k in range(1, XN):
        o2_arrival(k).wait_recv()
        o3_copy(k).start()
    head = hdbuf[rem(x, 2), lax.div(x, jnp.int32(2))]
    for k in range(1, XN):
        q = x_peer(XN - k)
        sc_arrival(k).wait_recv()
        o3_arrival(k).wait_recv()
        scale, shrink = columns(screcv[q])
        wide = o2buf[q].reshape(N, F).astype(jnp.float32)
        go2buf[q] = (scale * head - shrink * wide).astype(jnp.bfloat16)
    tokens = XN * N
    tile = min(128, H)

    def down_weight_step(i):
        rows = span(i, tile)
        dd_ref[rows, :] = dot(ht[rows, :], go2buf[...].reshape(tokens, F)).astype(jnp.bfloat16)

    loop(H // tile, down_weight_step)

    def gg_of(s):
        grad = ghbuf[s].astype(jnp.float32)
        ggbuf[s, :, 0:H] = (grad * coef[s, :, 0:H]).astype(jnp.bfloat16)
        ggbuf[s, :, H:2 * H] = (grad * coef[s, :, H:2 * H]).astype(jnp.bfloat16)

    gg_of(my_seat)

    def gg_step(k):
        q = row_peer(k)
        gh_arrival(q).wait_recv()
        gg_of(seat(q))

    loop(R, gg_step, 1)

    tile_f = min(128, F)

    def weight_step(i):
        rows = span(i, tile_f)
        both = dot(y2t[rows, :], ggbuf[...].reshape(tokens, 2 * H)).astype(jnp.bfloat16)
        dg_ref[rows, :] = both[:, 0:H]
        du_ref[rows, :] = both[:, H:2 * H]

    loop(F // tile_f, weight_step)

    for k in range(1, R):
        gvo_arrival(row_peer(k)).wait_recv()
    head_sum = grecv[side * XN]
    for k in range(1, XN):
        head_sum = head_sum + grecv[side * XN + k]
    pick = lax.broadcasted_iota(jnp.int32, head_sum.shape, 0) == c - side * XN
    gval_ref[...] = jnp.sum(jnp.where(pick, head_sum, 0.0), axis=0, keepdims=True)

    gx.drain()
    ga.drain()
    for j in range(YH):
        @pl.when((yl == 0) & jnp.logical_not(home & (yh == j)))
        def _():
            gn_copy(j).wait_send()
            hd_copy(j).wait_send()
    gb_copy.wait_send()
    hb_copy.wait_send()
    t1_copy.wait_send()
    rs_copy.wait_send()
    q2_copy.wait_send()
    g1_copy.wait_send()

    w_drain(gate_w, up_w, down_w)
    h_copy.wait_send()
    gp_copy.wait_send()

    def x_sends(k):
        y2_copy(k).wait_send()
        gu_copy(k).wait_send()
        yb_copy(k).wait_send()
        o2_copy(k).wait_send()
        o3_copy(k).wait_send()
        sc_copy(k).wait_send()

    loop(XN, x_sends, 1)

    def row_sends(k):
        q = row_peer(k)
        q1_copy(q).wait_send()
        gh_copy(q).wait_send()
        gvo_copy(q).wait_send()

    loop(R, row_sends, 1)

    def depth_sends(k):
        t2_copy(k).wait_send()
        za_copy(depth_peer(k)).wait_send()
        zb2_copy(depth_peer(k)).wait_send()

    loop(Z, depth_sends, 1)
    for s in range(2):
        ob_copy(s).wait_send()
        for m in range(YQ):
            @pl.when(jnp.logical_not(is_owner(s, m)))
            def _():
                ya_copy(s, m).wait_send()
                yb2_copy(s, m).wait_send()


def hand_out(
    dg_ref, du_ref, dd_ref, val_ref, gval_ref,
    dg_out, du_out, dd_out, val_out, gval_out,
    dg_buf, du_buf, dd_buf, fetched, stored,
):
    parts = ((dg_ref, dg_buf, dg_out), (du_ref, du_buf, du_out), (dd_ref, dd_buf, dd_out))
    reads = [
        pltpu.make_async_copy(src, buf, fetched.at[i]) for i, (src, buf, _) in enumerate(parts)
    ]
    writes = [
        pltpu.make_async_copy(buf, dst, stored.at[i]) for i, (_, buf, dst) in enumerate(parts)
    ]
    for one in reads:
        one.start()
    val_out[...] = val_ref[:, 0:val_out.shape[1]]
    gval_out[...] = gval_ref[...]
    for read, write in zip(reads, writes):
        read.wait()
        write.start()
    for one in writes:
        one.wait()


def build(mesh):
    R, C, Z = mesh.shape["row"], mesh.shape["col"], mesh.shape["depth"]
    YH, XN = C // 2, R // 2
    YQ = YH // 2

    def per_device(residual, pre_gain, w_gate, w_up, w_down, value_head, sample_index, return_table):
        B, F = residual.shape
        H = w_gate.shape[1]
        N = Z * 2 * B
        L = N // 2
        entries = return_table.shape[0]

        bf, f32 = jnp.bfloat16, jnp.float32
        V = pltpu.VMEM
        dma = lambda *shape: pltpu.SemaphoreType.DMA(shape)
        F2 = F // 2
        gather = [
            dma(YH), dma(2 * YQ), dma(Z), dma(Z), dma(Z), dma(Z),
            dma(Z), dma(Z), dma(YH), dma(2 * YQ), dma(2 * YQ), dma(2 * YQ),
        ]
        scratch = [
            V((2, YQ, Z, 2, B, F), bf), V((Z, B, F2), bf),
            V((XN, N, F), bf), V((XN, N, F), bf), V((F, XN * N), bf),
            V((XN, F, H), bf), V((XN, F, H), bf), V((XN, H, F), bf),
            V((2, YQ, 1, F), f32), V((2, YQ, 1, F), f32), V((B, F), bf),
            pltpu.SMEM((1, B), jnp.int32), V((entries // 128, 128), f32),
            V((8, L), f32), V((8, L), f32), V((8, L), f32), V((Z, 8, L), f32),
            V((N, 2 * H), f32), V((2, N, 128), f32), V((L, 2 * H), bf), V((L, 2 * H), bf),
            V((8, L), f32), V((R, 8, L), f32),
            V((2, L, H), bf), V((H, R * L), bf), V((R, L, 2 * H), bf), V((R, L, 2 * H), f32),
            V((YQ, N, F), bf), V((YQ, N, F), bf), V((YQ, N, F), f32),
            V((YQ, Z, 2, B, F), bf), V((Z, YQ, 2, B, F2), bf), V((YH, B, F2), bf),
            V((YH, Z, B, F2), bf), V((Z, B, F2), bf), V((YQ, 2, B, F2), bf), V((Z, B, F2), bf),
            V((B, F), bf), V((2, YQ, Z, 2, B, F), bf), V((Z, B, F2), bf),
            V((8, L), f32), V((8, L), f32), V((8, L), f32), V((XN, 8, L), f32),
            V((XN, Z, 2, B, F), bf), V((XN, N, F), bf), V((XN, N, F), bf),
            V((N, H), f32), V((L, H), bf), V((L, H), bf),
            V((R, L, H), bf), V((R, L, 2 * H), bf), V((8, F), f32), V((R, 8, F), f32),
            *gather,
            dma(YH), dma(YQ), dma(YH), dma(YQ), dma(2), dma(2), dma(5), dma(), dma(), dma(Z), dma(Z),
            dma(3), dma(4), dma(4), dma(4), dma(4), dma(4), dma(4),
            dma(R), dma(R), dma(), dma(), dma(XN), dma(XN), dma(XN), dma(XN),
            dma(), dma(), dma(), dma(), dma(XN), dma(XN),
            dma(2), dma(2), dma(Z), dma(Z), dma(2 * YQ), dma(YH), dma(2 * YQ), dma(YH),
            dma(Z), dma(Z),
            *gather,
            dma(), dma(), dma(XN), dma(XN), dma(XN), dma(XN), dma(XN), dma(XN),
            dma(), dma(), dma(R), dma(R), dma(R), dma(R),
        ]
        vmem = pl.BlockSpec(memory_space=pltpu.VMEM)
        hbm = pl.BlockSpec(memory_space=pl.ANY)
        dg, du, dd, values, gval = pl.pallas_call(
            functools.partial(kernel, R, YH, Z, B, F, H),
            out_shape=(
                jax.ShapeDtypeStruct((F, H), bf),
                jax.ShapeDtypeStruct((F, H), bf),
                jax.ShapeDtypeStruct((H, F), bf),
                jax.ShapeDtypeStruct((1, 128), f32),
                jax.ShapeDtypeStruct((1, F), f32),
            ),
            in_specs=[hbm] * 8,
            out_specs=(vmem,) * 5,
            scratch_shapes=scratch,
            compiler_params=pltpu.CompilerParams(
                collective_id=0, has_side_effects=True, vmem_limit_bytes=VMEM_MB * 1024 * 1024
            ),
        )(
            residual, pre_gain.reshape(1, F), value_head.reshape(1, F),
            sample_index.reshape(1, B), return_table.reshape(entries // 128, 128),
            w_gate, w_up, w_down,
        )
        dg, du, dd, values, gval = pl.pallas_call(
            hand_out,
            out_shape=(
                jax.ShapeDtypeStruct((F, H), bf),
                jax.ShapeDtypeStruct((F, H), bf),
                jax.ShapeDtypeStruct((H, F), bf),
                jax.ShapeDtypeStruct((1, B), f32),
                jax.ShapeDtypeStruct((1, F), f32),
            ),
            in_specs=[hbm, hbm, hbm, vmem, vmem],
            out_specs=(hbm, hbm, hbm, vmem, vmem),
            scratch_shapes=[V((F, H), bf), V((F, H), bf), V((H, F), bf), dma(3), dma(3)],
        )(dg, du, dd, values, gval)
        return values.reshape(B), dg, du, dd, gval.reshape(F)

    return per_device


def solution(mesh):
    placed = (
        P(("row", "depth"), "col"),
        P("col"),
        P("row", ("col", "depth")),
        P("row", ("col", "depth")),
        P(("col", "depth"), "row"),
        P("col"),
        P(("row", "depth")),
        P(),
    )
    return jax.shard_map(
        build(mesh),
        mesh=mesh,
        in_specs=placed,
        out_specs=(
            P(("row", "depth")),
            P("row", ("col", "depth")),
            P("row", ("col", "depth")),
            P(("col", "depth"), "row"),
            P("col"),
        ),
        check_vma=False,
    )
```

```python
import functools

import jax
import jax.numpy as jnp
from jax import lax
from jax.experimental import pallas as pl
from jax.experimental.pallas import tpu as pltpu
from jax.sharding import PartitionSpec as P

MESH = pl.DeviceIdType.MESH
norm_eps = 1e-06
huber_delta = 1.0
VMEM_MB = 56


def rem(value, size):
    return lax.rem(value, jnp.int32(size))


def dot(left, right):
    return jnp.dot(left, right, preferred_element_type=jnp.float32)


def dot_t(left, right):
    return lax.dot_general(
        left, right, (((1,), (1,)), ((), ())), preferred_element_type=jnp.float32
    )


def kernel(
    R, YH, Z, B, F, H,
    x_ref, gain_ref, head_ref, index_ref, table_ref, wg_ref, wu_ref, wd_ref,
    dg_ref, du_ref, dd_ref, val_ref, gval_ref,
    xbuf, xzb, ybuf, y2buf, y2t, wgbuf, wubuf, wdbuf, gnbuf, hdbuf, xblk, index, table,
    tgown, tg1, tgsend, tg2,
    acc, stat, rssend, rsrecv, st1send, st1recv, hbuf, ht, gubuf, coef,
    osend, osib, oown, zsend, zra, yra, yrb, zrb, ysa, zsb, outblk, obuf, ozb,
    st2send, st2recv, scsend, screcv, o2buf, gobuf, go2buf,
    ghpart, ghsend, ghrecv, ghbuf, ggbuf, gsum, grecv,
    x1, x2, x3, x4, x5, x6, x7, x8, x9, x10, x11, x12, gvs, gvr, hds, hdr, gbs, gbr, los, t1s, t1r, t2s, t2r,
    wls, wgs, wgr, wus, wur, wds, wdr, q1s, q1r, rss, rsr, y2s, y2r, ybs, ybr, hs, hr, gps, gpr, gus, gur,
    obs, obr, zas, zar, yas, yar, ybbs, ybbr, zbs, zbr,
    a1, a2, a3, a4, a5, a6, a7, a8, a9, a10, a11, a12, q2s, q2r, scs, scr,
    o2s, o2r, o3s, o3r, g1s, g1r, ghs, ghr, gvos, gvor,
):
    XN, YQ = R // 2, YH // 2
    N = Z * 2 * B
    L = N // 2
    features = R * F
    F2 = F // 2
    ZH = Z // 2
    lo, hi = pl.ds(0, F2), pl.ds(F2, F2)
    r = lax.axis_index("row")
    c = lax.axis_index("col")
    d = lax.axis_index("depth")
    x = rem(r, XN)
    yl = lax.div(r, jnp.int32(XN))
    core = rem(c, 2)
    yh = lax.div(c, jnp.int32(2))
    side = lax.div(yh, jnp.int32(YQ))
    mloc = rem(yh, YQ)
    home = yl == side
    sibling = (r, 2 * yh + 1 - core, d)
    ypair = ((1 - yl) * XN + x, c, d)

    def copy(src, dst, send, recv, device):
        return pltpu.make_async_remote_copy(
            src_ref=src, dst_ref=dst, send_sem=send, recv_sem=recv,
            device_id=device, device_id_type=MESH,
        )

    def row_peer(k):
        return rem(r + k, R)

    def depth_peer(k):
        return rem(d + k, Z)

    def x_peer(k):
        return rem(x + k, XN)

    def row_device(q):
        return (q, c, d)

    def depth_device(q):
        return (r, c, q)

    def x_device(q):
        return (yl * XN + q, c, d)

    def seat(q):
        return rem(q, XN) * 2 + lax.div(q, jnp.int32(XN))

    my_seat = x * 2 + yl

    def reader(j):
        return (side * XN + x, 2 * j + core, d)

    def owner(s, m):
        return (s * XN + x, 2 * (yl * YQ + m) + core, d)

    def is_owner(s, m):
        return (yl == s) & (yh == yl * YQ + m)

    def span(index, size):
        return pl.ds(pl.multiple_of(index * size, size), size)

    def loop(count, body, start=0):
        def step(k, carry):
            body(k)
            return carry
        lax.fori_loop(start, count, step, 0)

    eye = (
        lax.broadcasted_iota(jnp.int32, (L, L), 0)
        == lax.broadcasted_iota(jnp.int32, (L, L), 1)
    )

    def to_lanes(column):
        return jnp.sum(jnp.where(eye, column, 0.0), axis=0, keepdims=True)

    def to_column(lanes):
        return jnp.sum(jnp.where(eye, lanes, 0.0), axis=1, keepdims=True)

    local_x = pltpu.make_async_copy(x_ref, xblk, los.at[0])
    local_index = pltpu.make_async_copy(index_ref, index, los.at[1])
    local_table = pltpu.make_async_copy(table_ref, table, los.at[2])
    for one in (local_x, local_index, local_table):
        one.start()

    barrier = pltpu.get_barrier_semaphore()

    def greet(device):
        pl.semaphore_signal(barrier, inc=1, device_id=device, device_id_type=MESH)

    for k in range(1, R):
        greet(row_device(row_peer(k)))
    for k in range(1, Z):
        greet(depth_device(depth_peer(k)))
    greet(sibling)
    for j in range(YH):
        @pl.when(jnp.logical_not(home & (yh == j)))
        def _():
            greet(reader(j))
    for s in range(2):
        for m in range(YQ):
            @pl.when(jnp.logical_not(is_owner(s, m)))
            def _():
                greet(owner(s, m))
    pl.semaphore_wait(
        barrier, (R - 1) + (Z - 1) + 1 + YH + 2 * YQ - jnp.where(home, 2, 0)
    )

    near = []
    for k in range(1, Z // 2 + 1):
        near.append(k)
        if Z - k > k:
            near.append(Z - k)

    class Gather:
        def __init__(self, src, local, buf, zb, *sems):
            self.src, self.local, self.buf, self.zb = src, local, buf, zb
            (self.ays, self.ayr, self.azs, self.azr, self.ass, self.asr,
             self.bzs, self.bzr, self.bys, self.byr, self.bss, self.bsr) = sems

        def ay_copy(self, j):
            return copy(
                self.src.at[:, lo], self.buf.at[core, mloc, d, yl, :, lo],
                self.ays.at[j], self.ayr.at[yl * YQ + mloc], reader(j),
            )

        def ay_arrival(self, s, m):
            return copy(
                self.src.at[:, lo], self.buf.at[core, m, d, s, :, lo],
                self.ays.at[0], self.ayr.at[s * YQ + m], owner(s, m),
            )

        def az_copy(self, k):
            part = self.buf.at[core, :, d, :, :, lo]
            return copy(
                part, part, self.azs.at[k], self.azr.at[k], depth_device(depth_peer(k))
            )

        def az_arrival(self, k):
            q = depth_peer(Z - k)
            part = self.buf.at[core, :, q, :, :, lo]
            return copy(part, part, self.azs.at[k], self.azr.at[k], depth_device(q))

        def as_copy(self, k):
            part = self.buf.at[core, :, depth_peer(Z - k), :, :, lo]
            return copy(part, part, self.ass.at[k], self.asr.at[k], sibling)

        def as_arrival(self, k):
            part = self.buf.at[1 - core, :, depth_peer(Z - k), :, :, lo]
            return copy(part, part, self.ass.at[k], self.asr.at[k], sibling)

        def bz_copy(self, k):
            return copy(
                self.src.at[:, hi], self.zb.at[d], self.bzs.at[k], self.bzr.at[k],
                depth_device(depth_peer(k)),
            )

        def bz_arrival(self, k):
            q = depth_peer(Z - k)
            return copy(
                self.src.at[:, hi], self.zb.at[q], self.bzs.at[k], self.bzr.at[k],
                depth_device(q),
            )

        def by_copy(self, j):
            return copy(
                self.zb, self.buf.at[core, mloc, :, yl, :, hi],
                self.bys.at[j], self.byr.at[yl * YQ + mloc], reader(j),
            )

        def by_arrival(self, s, m):
            return copy(
                self.zb, self.buf.at[core, m, :, s, :, hi],
                self.bys.at[0], self.byr.at[s * YQ + m], owner(s, m),
            )

        def bs_copy(self, s, m):
            part = self.buf.at[core, m, :, s, :, hi]
            i = s * YQ + m
            return copy(part, part, self.bss.at[i], self.bsr.at[i], sibling)

        def bs_arrival(self, s, m):
            part = self.buf.at[1 - core, m, :, s, :, hi]
            i = s * YQ + m
            return copy(part, part, self.bss.at[i], self.bsr.at[i], sibling)

        def start(self):
            for j in range(YH):
                @pl.when(jnp.logical_not(home & (yh == j)))
                def _():
                    self.ay_copy(j).start()
            for k in reversed(near):
                self.bz_copy(k).start()

        def keep(self):
            @pl.when(home)
            def _():
                self.buf[core, mloc, d, yl, :, 0:F2] = self.local[:, 0:F2]
            self.zb[d] = self.local[:, F2:F]

        def spread(self):
            for s in range(2):
                for m in range(YQ):
                    @pl.when(jnp.logical_not(is_owner(s, m)))
                    def _():
                        self.ay_arrival(s, m).wait_recv()
            for k in reversed(near):
                self.az_copy(k).start()
            self.as_copy(0).start()
            for k in near:
                self.bz_arrival(k).wait_recv()
            for j in range(YH):
                @pl.when(home & (yh == j))
                def _():
                    self.buf[core, mloc, :, yl, :, F2:F] = self.zb[...]

                @pl.when(jnp.logical_not(home & (yh == j)))
                def _():
                    self.by_copy(j).start()

        def pass_on(self, ks):
            for k in ks:
                self.az_arrival(k).wait_recv()
                self.as_copy(k).start()

        def pass_on_upper(self):
            for s in range(2):
                for m in range(YQ):
                    @pl.when(jnp.logical_not(is_owner(s, m)))
                    def _():
                        self.by_arrival(s, m).wait_recv()
                    self.bs_copy(s, m).start()

        def arrived(self):
            for k in [0] + near:
                self.as_arrival(k).wait_recv()
            for s in range(2):
                for m in range(YQ):
                    self.bs_arrival(s, m).wait_recv()

        def drain(self):
            for j in range(YH):
                @pl.when(jnp.logical_not(home & (yh == j)))
                def _():
                    self.ay_copy(j).wait_send()
                    self.by_copy(j).wait_send()
            for k in range(1, Z):
                self.az_copy(k).wait_send()
                self.bz_copy(k).wait_send()
            for k in range(Z):
                self.as_copy(k).wait_send()
            for s in range(2):
                for m in range(YQ):
                    self.bs_copy(s, m).wait_send()

    gx = Gather(x_ref, xblk, xbuf, xzb, x1, x2, x3, x4, x5, x6, x7, x8, x9, x10, x11, x12)
    gx.start()

    def gn_copy(j):
        return copy(gain_ref, gnbuf.at[core, mloc], gvs.at[j], gvr.at[mloc], reader(j))

    def hd_copy(j):
        return copy(head_ref, hdbuf.at[core, mloc], hds.at[j], hdr.at[mloc], reader(j))

    def gn_arrival(m):
        return copy(gain_ref, gnbuf.at[core, m], gvs.at[0], gvr.at[m], owner(0, m))

    def hd_arrival(m):
        return copy(head_ref, hdbuf.at[core, m], hds.at[0], hdr.at[m], owner(0, m))

    gn_local = pltpu.make_async_copy(gain_ref, gnbuf.at[core, mloc], los.at[3])
    hd_local = pltpu.make_async_copy(head_ref, hdbuf.at[core, mloc], los.at[4])

    @pl.when((yl == 0) & home)
    def _():
        gn_local.start()
        hd_local.start()

    for j in range(YH):
        @pl.when((yl == 0) & jnp.logical_not(home & (yh == j)))
        def _():
            gn_copy(j).start()
            hd_copy(j).start()

    def local_weights():
        return (
            pltpu.make_async_copy(wg_ref, wgbuf.at[x], wls.at[0]),
            pltpu.make_async_copy(wu_ref, wubuf.at[x], wls.at[1]),
            pltpu.make_async_copy(wd_ref, wdbuf.at[x], wls.at[2]),
        )

    for one in local_weights():
        one.start()

    def half_rows(ref, k, i):
        rows = ref.shape[0] // 2
        return pl.ds(rows * ((0 if k == 1 else 1) ^ i), rows)

    def w_copy(ref, buf, send, recv, k, i):
        rows = half_rows(ref, k, i)
        return copy(
            ref.at[rows], buf.at[x, rows], send.at[2 * k + i], recv.at[2 * k + i],
            x_device(x_peer(k)),
        )

    def w_arrival(ref, buf, send, recv, k, i):
        q = x_peer(XN - k)
        rows = half_rows(ref, k, i)
        return copy(
            ref.at[rows], buf.at[q, rows], send.at[2 * k + i], recv.at[2 * k + i], x_device(q)
        )

    def w_onward(ref, buf, send, recv, k):
        part = buf.at[x_peer(XN - k), half_rows(ref, k, 0)]
        return copy(part, part, send.at[2 * (k - 1)], recv.at[2 * (k - 1)], x_device(x_peer(k)))

    def w_onward_arrival(ref, buf, send, recv, k):
        part = buf.at[x_peer(2), half_rows(ref, k, 0)]
        return copy(part, part, send.at[2 * (k - 1)], recv.at[2 * (k - 1)], x_device(x_peer(XN - k)))

    gate_w = (wg_ref, wgbuf, wgs, wgr)
    up_w = (wu_ref, wubuf, wus, wur)
    down_w = (wd_ref, wdbuf, wds, wdr)
    sides = (1,) if XN == 2 else (1, 3)

    def w_start(*which):
        for i in range(2):
            for k in sides:
                for w in which:
                    w_copy(*w, k, i).start()

    def w_turn(*which):
        for k in sides:
            for w in which:
                w_arrival(*w, k, 0).wait_recv()
                if XN == 4:
                    w_onward(*w, k).start()

    def w_finish(*which):
        for k in sides:
            for w in which:
                w_arrival(*w, k, 1).wait_recv()
        if XN == 4:
            for k in sides:
                for w in which:
                    w_onward_arrival(*w, k).wait_recv()

    def w_drain(*which):
        for k in sides:
            for w in which:
                w_copy(*w, k, 0).wait_send()
                w_copy(*w, k, 1).wait_send()
                if XN == 4:
                    w_onward(*w, k).wait_send()

    w_start(gate_w, up_w)

    local_x.wait()
    gx.keep()

    local_index.wait()
    local_table.wait()
    place = d * (2 * B) + yl * B
    place_row = lax.div(place, jnp.int32(L))
    place_lane = rem(place, L)
    table_lanes = lax.broadcasted_iota(jnp.int32, (1, 128), 1)
    lanes = lax.broadcasted_iota(jnp.int32, (1, L), 1)

    def look_up(i, found):
        entry = index[0, i]
        line = table[pl.ds(lax.div(entry, jnp.int32(128)), 1), :]
        value = jnp.sum(
            jnp.where(table_lanes == rem(entry, 128), line, 0.0), axis=1, keepdims=True
        )
        return found + jnp.where(lanes == place_lane + i, value, 0.0)

    found = lax.fori_loop(0, B, look_up, jnp.zeros((1, L), jnp.float32))
    tile_rows = lax.broadcasted_iota(jnp.int32, (8, L), 0)
    tgown[...] = jnp.where(tile_rows == place_row, found, 0.0)
    t1_copy = copy(tgown, tg1, t1s, t1r, ypair)
    t1_copy.start()

    gx.spread()

    for m in range(YQ):
        here = (yl == 0) & is_owner(0, m)

        @pl.when(here)
        def _():
            gn_local.wait()
            hd_local.wait()

        @pl.when(jnp.logical_not(here))
        def _():
            gn_arrival(m).wait_recv()
            hd_arrival(m).wait_recv()
    gb_copy = copy(gnbuf.at[core], gnbuf.at[core], gbs.at[0], gbr.at[0], sibling)
    hb_copy = copy(hdbuf.at[core], hdbuf.at[core], gbs.at[1], gbr.at[1], sibling)
    gb_arrival = copy(gnbuf.at[1 - core], gnbuf.at[1 - core], gbs.at[0], gbr.at[0], sibling)
    hb_arrival = copy(hdbuf.at[1 - core], hdbuf.at[1 - core], gbs.at[1], gbr.at[1], sibling)
    gb_copy.start()
    hb_copy.start()

    t1_copy.wait_recv()
    tgsend[...] = tgown[...] + tg1[...]

    def t2_copy(k):
        return copy(tgsend, tg2.at[d], t2s.at[k], t2r.at[k], depth_device(depth_peer(k)))

    def t2_arrival(k):
        q = depth_peer(Z - k)
        return copy(tgsend, tg2.at[q], t2s.at[k], t2r.at[k], depth_device(q))

    for k in range(1, Z):
        t2_copy(k).start()

    w_turn(gate_w, up_w)
    w_start(down_w)
    gx.pass_on(near)
    gx.pass_on_upper()
    for one in local_weights():
        one.wait()

    def fold(wide):
        total = wide[:, 0:128]
        for i in range(1, F // 128):
            total = total + wide[:, 128 * i:128 * (i + 1)]
        return total

    def lane_sums(folded):
        column = jnp.sum(folded, axis=1, keepdims=True)
        return [to_lanes(column[s * L:(s + 1) * L]) for s in range(2)]

    def gate_up(which, m):
        fl = 2 * m + which
        wide = xbuf[which, m].reshape(N, F).astype(jnp.float32)
        scaled = (wide * gnbuf[which, m]).astype(jnp.bfloat16)
        ybuf[fl] = scaled
        acc[:, 0:H] += dot(scaled, wgbuf[fl])
        acc[:, H:2 * H] += dot(scaled, wubuf[fl])
        stat[0] += fold(wide * wide)

    acc[...] = jnp.zeros_like(acc)
    stat[...] = jnp.zeros_like(stat)
    w_finish(gate_w, up_w)
    loop(YQ, lambda m: gate_up(core, m))
    w_turn(down_w)
    gb_arrival.wait_recv()
    gx.arrived()
    loop(YQ, lambda m: gate_up(1 - core, m))

    rs_copy = copy(rssend, rsrecv, rss, rsr, ypair)
    rssend[...] = acc[span(1 - yl, L)].astype(jnp.bfloat16)

    def q1_copy(q):
        return copy(st1send, st1recv.at[r], q1s.at[q], q1r.at[r], row_device(q))

    def q1_arrival(q):
        return copy(st1send, st1recv.at[q], q1s.at[q], q1r.at[q], row_device(q))

    pair_row = (1 - yl) * XN + x
    st1send[...] = jnp.concatenate(lane_sums(stat[0]) * 4, axis=0)
    q1_copy(pair_row).start()
    rs_copy.start()
    for k in range(1, R):
        q = row_peer(k)

        @pl.when(q != pair_row)
        def _():
            q1_copy(q).start()
    st1recv[r] = st1send[...]

    near_half = span(core, L)
    far_half = span(1 - core, L)

    def y2_copy(k):
        q = x_peer(k)
        return copy(
            ybuf.at[q, near_half], y2buf.at[x, near_half], y2s.at[k], y2r.at[k], x_device(q)
        )

    def y2_arrival(k):
        q = x_peer(XN - k)
        part = y2buf.at[q, near_half]
        return copy(part, part, y2s.at[k], y2r.at[k], x_device(q))

    def yb_copy(k):
        part = y2buf.at[x_peer(XN - k), near_half]
        return copy(part, part, ybs.at[k], ybr.at[k], sibling)

    def yb_arrival(k):
        part = y2buf.at[x_peer(XN - k), far_half]
        return copy(part, part, ybs.at[k], ybr.at[k], sibling)

    for k in range(1, XN):
        y2_copy(k).start()

    q1_arrival(pair_row).wait_recv()
    squares = st1send[...] + st1recv[pair_row]
    inv_lanes = lax.rsqrt(squares / features + norm_eps)
    inv_mine = jnp.where(yl == 0, inv_lanes[0:1, :], inv_lanes[1:2, :])
    inv_norm = to_column(inv_mine)
    rs_copy.wait_recv()
    total = (acc[span(yl, L)] + rsrecv[...].astype(jnp.float32)) * inv_norm
    gate, up = total[:, 0:H], total[:, H:2 * H]
    hbuf[yl] = (gate * jax.nn.sigmoid(gate) * up).astype(jnp.bfloat16)

    h_copy = copy(hbuf.at[yl], hbuf.at[yl], hs, hr, ypair)
    h_arrival = copy(hbuf.at[1 - yl], hbuf.at[1 - yl], hs, hr, ypair)

    gp_copy = copy(gubuf.at[my_seat], gubuf.at[my_seat], gps, gpr, ypair)
    pair_seat = x * 2 + 1 - yl
    gp_arrival = copy(gubuf.at[pair_seat], gubuf.at[pair_seat], gps, gpr, ypair)

    def gu_copy(k):
        part = gubuf.at[pl.ds(x * 2, 2)]
        return copy(part, part, gus.at[k], gur.at[k], x_device(x_peer(k)))

    def gu_arrival(k):
        q = x_peer(XN - k)
        part = gubuf.at[pl.ds(q * 2, 2)]
        return copy(part, part, gus.at[k], gur.at[k], x_device(q))

    h_copy.start()
    gubuf[my_seat] = total.astype(jnp.bfloat16)

    w_finish(down_w)

    def ob_copy(s):
        part = pl.ds(pl.multiple_of(s * L, L), L)
        return copy(osend.at[:, part], osib.at[:, part], obs.at[s], obr.at[s], sibling)

    def down(s):
        rows = span(s, L)
        act = hbuf[s]
        for m in range(YQ):
            osend[m, rows] = dot(act, wdbuf[2 * m + 1 - core]).astype(jnp.bfloat16)
        ob_copy(s).start()
        for m in range(YQ):
            oown[m, rows] = dot(act, wdbuf[2 * m + core])

    down(yl)
    gp_copy.start()

    def za_copy(q):
        return copy(
            zsend.at[:, q, :, :, lo], zra.at[d], zas.at[q], zar.at[d], depth_device(q)
        )

    def za_arrival(q):
        return copy(
            zsend.at[:, q, :, :, lo], zra.at[q], zas.at[q], zar.at[q], depth_device(q)
        )

    def yb2_copy(s, m):
        return copy(
            zsend.at[m, :, s, :, hi], yrb.at[yh], ybbs.at[s * YQ + m], ybbr.at[yh], owner(s, m)
        )

    def yb2_arrival(j):
        return copy(
            zsend.at[0, :, 0, :, hi], yrb.at[j], ybbs.at[0], ybbr.at[j], reader(j)
        )

    def pair_sum(s):
        rows = span(s, L)
        ob_copy(s).wait_recv()
        for m in range(YQ):
            both = oown[m, rows] + osib[m, rows].astype(jnp.float32)
            oown[m, rows] = both
            zsend[m, pl.ds(s * ZH, ZH)] = both.astype(jnp.bfloat16).reshape(ZH, 2, B, F)
        for i in range(Z // 2):
            q = s * (Z // 2) + rem(d + i, Z // 2)

            @pl.when(q != d)
            def _():
                za_copy(q).start()

    pair_sum(yl)
    h_arrival.wait_recv()
    down(1 - yl)
    pair_sum(1 - yl)
    gp_arrival.wait_recv()
    for k in range(1, XN):
        gu_copy(k).start()

    for s in range(2):
        for m in range(YQ):
            @pl.when(is_owner(s, m))
            def _():
                yrb[yh] = zsend[m, :, s, :, F2:F]

            @pl.when(jnp.logical_not(is_owner(s, m)))
            def _():
                yb2_copy(s, m).start()

    y2t[:, span(x, N)] = ybuf[x].T

    mine = span(d, 2 * B)
    for k in near:
        q = depth_peer(k)
        za_arrival(q).wait_recv()
        for m in range(YQ):
            oown[m, mine, 0:F2] += zra[q, m].reshape(2 * B, F2).astype(jnp.float32)
    for m in range(YQ):
        ysa[m] = oown[m, mine, 0:F2].astype(jnp.bfloat16).reshape(2, B, F2)

    def ya_copy(s, m):
        return copy(
            ysa.at[m, s], yra.at[yh], yas.at[s * YQ + m], yar.at[yh], owner(s, m)
        )

    def ya_arrival(j):
        return copy(ysa.at[0, 0], yra.at[j], yas.at[0], yar.at[j], reader(j))

    for s in range(2):
        for m in range(YQ):
            @pl.when(is_owner(s, m))
            def _():
                yra[yh] = ysa[m, s]

            @pl.when(jnp.logical_not(is_owner(s, m)))
            def _():
                ya_copy(s, m).start()

    upper = jnp.zeros((Z, B, F2), jnp.float32)
    for j in range(YH):
        @pl.when(jnp.logical_not(home & (yh == j)))
        def _():
            yb2_arrival(j).wait_recv()
        upper = upper + yrb[j].astype(jnp.float32)
    zsb[...] = upper.astype(jnp.bfloat16)

    def zb2_copy(q):
        return copy(zsb.at[q], zrb.at[d], zbs.at[q], zbr.at[d], depth_device(q))

    def zb2_arrival(q):
        return copy(zsb.at[q], zrb.at[q], zbs.at[q], zbr.at[q], depth_device(q))

    for k in reversed(near):
        zb2_copy(depth_peer(k)).start()

    for k in range(1, XN):
        y2_arrival(k).wait_recv()
        yb_copy(k).start()

    output = xblk[:, 0:F2].astype(jnp.float32)
    for j in range(YH):
        @pl.when(jnp.logical_not(home & (yh == j)))
        def _():
            ya_arrival(j).wait_recv()
        output = output + yra[j].astype(jnp.float32)
    outblk[:, 0:F2] = output.astype(jnp.bfloat16)
    output = xblk[:, F2:F].astype(jnp.float32) + zsb[d].astype(jnp.float32)
    for k in near:
        q = depth_peer(k)
        zb2_arrival(q).wait_recv()
        output = output + zrb[q].astype(jnp.float32)
    outblk[:, F2:F] = output.astype(jnp.bfloat16)

    ga = Gather(outblk, outblk, obuf, ozb, a1, a2, a3, a4, a5, a6, a7, a8, a9, a10, a11, a12)
    ga.start()
    ga.keep()

    for k in range(1, XN):
        q = x_peer(XN - k)
        yb_arrival(k).wait_recv()
        y2t[:, span(q, N)] = y2buf[q].T

    ga.spread()

    def coef_of(q):
        s = seat(q)
        first = rem(q, XN)
        parity = lax.div(q, jnp.int32(XN))
        sums = st1recv[first] + st1recv[first + XN]
        lanes = jnp.where(parity == 0, sums[0:1, :], sums[1:2, :])
        inv = to_column(lax.rsqrt(lanes / features + norm_eps))
        both = gubuf[s].astype(jnp.float32)
        gate, up = both[:, 0:H], both[:, H:2 * H]
        sig = jax.nn.sigmoid(gate)
        coef[s, :, 0:H] = inv * (up * sig * (1.0 + gate * (1.0 - sig)))
        swish = gate * sig
        coef[s, :, H:2 * H] = inv * swish
        ht[:, span(s, L)] = (swish * up).astype(jnp.bfloat16).T

    for k in range(1, R):
        q = row_peer(k)

        @pl.when(q != pair_row)
        def _():
            q1_arrival(q).wait_recv()

    coef_of(x)
    coef_of(XN + x)

    def coef_step(k):
        gu_arrival(k).wait_recv()
        q = x_peer(XN - k)
        coef_of(q)
        coef_of(XN + q)

    loop(XN, coef_step, 1)

    ga.pass_on(near)
    ga.pass_on_upper()

    target = tgsend[...]
    for k in range(1, Z):
        t2_arrival(k).wait_recv()
        target = target + tg2[depth_peer(Z - k)]

    def stats(which, m):
        wide = obuf[which, m].reshape(N, F).astype(jnp.float32)
        stat[0] += fold(wide * wide)
        stat[1] += fold(wide * hdbuf[which, m])

    stat[...] = jnp.zeros_like(stat)
    loop(YQ, lambda m: stats(core, m))
    hb_arrival.wait_recv()
    ga.arrived()
    loop(YQ, lambda m: stats(1 - core, m))
    st2send[...] = jnp.concatenate((lane_sums(stat[0]) + lane_sums(stat[1])) * 2, axis=0)
    q2_copy = copy(st2send, st2recv, q2s, q2r, ypair)
    q2_copy.start()

    def o2_copy(k):
        q = x_peer(k)
        part = obuf.at[rem(q, 2), lax.div(q, jnp.int32(2)), pl.ds(core * ZH, ZH)]
        return copy(
            part, o2buf.at[x, pl.ds(core * ZH, ZH)], o2s.at[k], o2r.at[k], x_device(q)
        )

    def o2_arrival(k):
        q = x_peer(XN - k)
        part = o2buf.at[q, pl.ds(core * ZH, ZH)]
        return copy(part, part, o2s.at[k], o2r.at[k], x_device(q))

    def o3_copy(k):
        part = o2buf.at[x_peer(XN - k), pl.ds(core * ZH, ZH)]
        return copy(part, part, o3s.at[k], o3r.at[k], sibling)

    def o3_arrival(k):
        part = o2buf.at[x_peer(XN - k), pl.ds((1 - core) * ZH, ZH)]
        return copy(part, part, o3s.at[k], o3r.at[k], sibling)

    for k in range(1, XN):
        o2_copy(k).start()
    q2_copy.wait_recv()
    sums = st2send[...] + st2recv[...]
    inv_final = lax.rsqrt(sums[0:2] / features + norm_eps)
    values = sums[2:4] * inv_final
    value_row = jnp.where(place_row == 0, values[0:1], values[1:2])
    own_values = jnp.sum(
        jnp.where(
            lax.broadcasted_iota(jnp.int32, (B, L), 1)
            == place_lane + lax.broadcasted_iota(jnp.int32, (B, L), 0),
            value_row, 0.0,
        ),
        axis=1, keepdims=True,
    )
    val_ref[...] = jnp.sum(
        jnp.where(
            lax.broadcasted_iota(jnp.int32, (B, B), 1)
            == lax.broadcasted_iota(jnp.int32, (B, B), 0),
            own_values, 0.0,
        ),
        axis=0, keepdims=True,
    )
    slope = jnp.clip(values - target[0:2], -huber_delta, huber_delta)
    scale_lanes = inv_final * slope
    shrink_lanes = inv_final * inv_final * (slope * values / features)
    scsend[...] = jnp.concatenate([scale_lanes, shrink_lanes] * 2, axis=0)

    def sc_copy(k):
        return copy(scsend, screcv.at[x], scs.at[k], scr.at[k], x_device(x_peer(k)))

    def sc_arrival(k):
        q = x_peer(XN - k)
        return copy(scsend, screcv.at[q], scs.at[k], scr.at[k], x_device(q))

    for k in range(1, XN):
        sc_copy(k).start()

    def columns(lanes):
        return (
            jnp.concatenate([to_column(lanes[0:1]), to_column(lanes[1:2])], axis=0),
            jnp.concatenate([to_column(lanes[2:3]), to_column(lanes[3:4])], axis=0),
        )

    scale, shrink = columns(scsend[...])

    gsum[...] = jnp.zeros_like(gsum)
    ghpart[...] = jnp.zeros_like(ghpart)

    def grad_output(fl):
        which = rem(fl, 2)
        m = lax.div(fl, jnp.int32(2))
        wide = obuf[which, m].reshape(N, F).astype(jnp.float32)
        head = hdbuf[which, m]
        gobuf[fl] = (scale * head - shrink * wide).astype(jnp.bfloat16)
        gsum[pl.ds(fl, 1), :] = jnp.sum(wide * scale, axis=0, keepdims=True)
        ghpart[...] += dot_t(gobuf[fl], wdbuf[fl])

    loop(XN, grad_output)

    g1_copy = copy(ghsend, ghrecv, g1s, g1r, ypair)
    ghsend[...] = ghpart[span(1 - yl, L)].astype(jnp.bfloat16)
    g1_copy.start()

    def gvo_copy(q):
        return copy(gsum, grecv.at[r], gvos.at[q], gvor.at[r], row_device(q))

    def gvo_arrival(q):
        return copy(gsum, grecv.at[q], gvos.at[q], gvor.at[q], row_device(q))

    def gh_copy(q):
        part = ghbuf.at[my_seat]
        return copy(part, part, ghs.at[q], ghr.at[r], row_device(q))

    def gh_arrival(q):
        part = ghbuf.at[seat(q)]
        return copy(part, part, ghs.at[q], ghr.at[q], row_device(q))

    g1_copy.wait_recv()
    ghbuf[my_seat] = (
        ghpart[span(yl, L)] + ghrecv[...].astype(jnp.float32)
    ).astype(jnp.bfloat16)
    for k in range(1, R):
        gh_copy(row_peer(k)).start()
    for k in range(1, R):
        gvo_copy(row_peer(k)).start()
    grecv[r] = gsum[...]

    go2buf[x] = gobuf[x]
    for k in range(1, XN):
        o2_arrival(k).wait_recv()
        o3_copy(k).start()
    head = hdbuf[rem(x, 2), lax.div(x, jnp.int32(2))]
    for k in range(1, XN):
        q = x_peer(XN - k)
        sc_arrival(k).wait_recv()
        o3_arrival(k).wait_recv()
        scale, shrink = columns(screcv[q])
        wide = o2buf[q].reshape(N, F).astype(jnp.float32)
        go2buf[q] = (scale * head - shrink * wide).astype(jnp.bfloat16)
    tokens = XN * N
    tile = min(128, H)

    def down_weight_step(i):
        rows = span(i, tile)
        dd_ref[rows, :] = dot(ht[rows, :], go2buf[...].reshape(tokens, F)).astype(jnp.bfloat16)

    loop(H // tile, down_weight_step)

    def gg_of(s):
        grad = ghbuf[s].astype(jnp.float32)
        ggbuf[s, :, 0:H] = (grad * coef[s, :, 0:H]).astype(jnp.bfloat16)
        ggbuf[s, :, H:2 * H] = (grad * coef[s, :, H:2 * H]).astype(jnp.bfloat16)

    gg_of(my_seat)

    def gg_step(k):
        q = row_peer(k)
        gh_arrival(q).wait_recv()
        gg_of(seat(q))

    loop(R, gg_step, 1)

    tile_f = min(128, F)

    def weight_step(i):
        rows = span(i, tile_f)
        both = dot(y2t[rows, :], ggbuf[...].reshape(tokens, 2 * H)).astype(jnp.bfloat16)
        dg_ref[rows, :] = both[:, 0:H]
        du_ref[rows, :] = both[:, H:2 * H]

    loop(F // tile_f, weight_step)

    for k in range(1, R):
        gvo_arrival(row_peer(k)).wait_recv()
    head_sum = grecv[side * XN]
    for k in range(1, XN):
        head_sum = head_sum + grecv[side * XN + k]
    pick = lax.broadcasted_iota(jnp.int32, head_sum.shape, 0) == c - side * XN
    gval_ref[...] = jnp.sum(jnp.where(pick, head_sum, 0.0), axis=0, keepdims=True)

    gx.drain()
    ga.drain()
    for j in range(YH):
        @pl.when((yl == 0) & jnp.logical_not(home & (yh == j)))
        def _():
            gn_copy(j).wait_send()
            hd_copy(j).wait_send()
    gb_copy.wait_send()
    hb_copy.wait_send()
    t1_copy.wait_send()
    rs_copy.wait_send()
    q2_copy.wait_send()
    g1_copy.wait_send()

    w_drain(gate_w, up_w, down_w)
    h_copy.wait_send()
    gp_copy.wait_send()

    def x_sends(k):
        y2_copy(k).wait_send()
        gu_copy(k).wait_send()
        yb_copy(k).wait_send()
        o2_copy(k).wait_send()
        o3_copy(k).wait_send()
        sc_copy(k).wait_send()

    loop(XN, x_sends, 1)

    def row_sends(k):
        q = row_peer(k)
        q1_copy(q).wait_send()
        gh_copy(q).wait_send()
        gvo_copy(q).wait_send()

    loop(R, row_sends, 1)

    def depth_sends(k):
        t2_copy(k).wait_send()
        za_copy(depth_peer(k)).wait_send()
        zb2_copy(depth_peer(k)).wait_send()

    loop(Z, depth_sends, 1)
    for s in range(2):
        ob_copy(s).wait_send()
        for m in range(YQ):
            @pl.when(jnp.logical_not(is_owner(s, m)))
            def _():
                ya_copy(s, m).wait_send()
                yb2_copy(s, m).wait_send()


def hand_out(*refs):
    sources, targets, buffers = refs[0:5], refs[5:10], refs[10:15]
    fetched, stored = refs[15:]
    reads = [
        pltpu.make_async_copy(src, buf, fetched.at[i])
        for i, (src, buf) in enumerate(zip(sources, buffers))
    ]
    writes = [
        pltpu.make_async_copy(buf, dst, stored.at[i])
        for i, (buf, dst) in enumerate(zip(buffers, targets))
    ]
    for one in reads:
        one.start()
    for read, write in zip(reads, writes):
        read.wait()
        write.start()
    for one in writes:
        one.wait()


def build(mesh):
    R, C, Z = mesh.shape["row"], mesh.shape["col"], mesh.shape["depth"]
    YH, XN = C // 2, R // 2
    YQ = YH // 2

    def per_device(residual, pre_gain, w_gate, w_up, w_down, value_head, sample_index, return_table):
        B, F = residual.shape
        H = w_gate.shape[1]
        N = Z * 2 * B
        L = N // 2
        entries = return_table.shape[0]

        bf, f32 = jnp.bfloat16, jnp.float32
        V = pltpu.VMEM
        dma = lambda *shape: pltpu.SemaphoreType.DMA(shape)
        F2 = F // 2
        gather = [
            dma(YH), dma(2 * YQ), dma(Z), dma(Z), dma(Z), dma(Z),
            dma(Z), dma(Z), dma(YH), dma(2 * YQ), dma(2 * YQ), dma(2 * YQ),
        ]
        scratch = [
            V((2, YQ, Z, 2, B, F), bf), V((Z, B, F2), bf),
            V((XN, N, F), bf), V((XN, N, F), bf), V((F, XN * N), bf),
            V((XN, F, H), bf), V((XN, F, H), bf), V((XN, H, F), bf),
            V((2, YQ, 1, F), f32), V((2, YQ, 1, F), f32), V((B, F), bf),
            pltpu.SMEM((1, B), jnp.int32), V((entries // 128, 128), f32),
            V((8, L), f32), V((8, L), f32), V((8, L), f32), V((Z, 8, L), f32),
            V((N, 2 * H), f32), V((2, N, 128), f32), V((L, 2 * H), bf), V((L, 2 * H), bf),
            V((8, L), f32), V((R, 8, L), f32),
            V((2, L, H), bf), V((H, R * L), bf), V((R, L, 2 * H), bf), V((R, L, 2 * H), f32),
            V((YQ, N, F), bf), V((YQ, N, F), bf), V((YQ, N, F), f32),
            V((YQ, Z, 2, B, F), bf), V((Z, YQ, 2, B, F2), bf), V((YH, B, F2), bf),
            V((YH, Z, B, F2), bf), V((Z, B, F2), bf), V((YQ, 2, B, F2), bf), V((Z, B, F2), bf),
            V((B, F), bf), V((2, YQ, Z, 2, B, F), bf), V((Z, B, F2), bf),
            V((8, L), f32), V((8, L), f32), V((8, L), f32), V((XN, 8, L), f32),
            V((XN, Z, 2, B, F), bf), V((XN, N, F), bf), V((XN, N, F), bf),
            V((N, H), f32), V((L, H), bf), V((L, H), bf),
            V((R, L, H), bf), V((R, L, 2 * H), bf), V((8, F), f32), V((R, 8, F), f32),
            *gather,
            dma(YH), dma(YQ), dma(YH), dma(YQ), dma(2), dma(2), dma(5), dma(), dma(), dma(Z), dma(Z),
            dma(3), dma(8), dma(8), dma(8), dma(8), dma(8), dma(8),
            dma(R), dma(R), dma(), dma(), dma(XN), dma(XN), dma(XN), dma(XN),
            dma(), dma(), dma(), dma(), dma(XN), dma(XN),
            dma(2), dma(2), dma(Z), dma(Z), dma(2 * YQ), dma(YH), dma(2 * YQ), dma(YH),
            dma(Z), dma(Z),
            *gather,
            dma(), dma(), dma(XN), dma(XN), dma(XN), dma(XN), dma(XN), dma(XN),
            dma(), dma(), dma(R), dma(R), dma(R), dma(R),
        ]
        vmem = pl.BlockSpec(memory_space=pltpu.VMEM)
        hbm = pl.BlockSpec(memory_space=pl.ANY)
        dg, du, dd, values, gval = pl.pallas_call(
            functools.partial(kernel, R, YH, Z, B, F, H),
            out_shape=(
                jax.ShapeDtypeStruct((F, H), bf),
                jax.ShapeDtypeStruct((F, H), bf),
                jax.ShapeDtypeStruct((H, F), bf),
                jax.ShapeDtypeStruct((1, B), f32),
                jax.ShapeDtypeStruct((1, F), f32),
            ),
            in_specs=[hbm] * 8,
            out_specs=(vmem,) * 5,
            scratch_shapes=scratch,
            compiler_params=pltpu.CompilerParams(
                collective_id=0, has_side_effects=True, vmem_limit_bytes=VMEM_MB * 1024 * 1024
            ),
        )(
            residual, pre_gain.reshape(1, F), value_head.reshape(1, F),
            sample_index.reshape(1, B), return_table.reshape(entries // 128, 128),
            w_gate, w_up, w_down,
        )
        dg, du, dd, values, gval = pl.pallas_call(
            hand_out,
            out_shape=(
                jax.ShapeDtypeStruct((F, H), bf),
                jax.ShapeDtypeStruct((F, H), bf),
                jax.ShapeDtypeStruct((H, F), bf),
                jax.ShapeDtypeStruct((1, B), f32),
                jax.ShapeDtypeStruct((1, F), f32),
            ),
            in_specs=[hbm] * 5,
            out_specs=(hbm,) * 5,
            scratch_shapes=[
                V((F, H), bf), V((F, H), bf), V((H, F), bf), V((1, B), f32), V((1, F), f32),
                dma(5), dma(5),
            ],
        )(dg, du, dd, values, gval)
        return values.reshape(B), dg, du, dd, gval.reshape(F)

    return per_device


def solution(mesh):
    placed = (
        P(("row", "depth"), "col"),
        P("col"),
        P("row", ("col", "depth")),
        P("row", ("col", "depth")),
        P(("col", "depth"), "row"),
        P("col"),
        P(("row", "depth")),
        P(),
    )
    return jax.shard_map(
        build(mesh),
        mesh=mesh,
        in_specs=placed,
        out_specs=(
            P(("row", "depth")),
            P("row", ("col", "depth")),
            P("row", ("col", "depth")),
            P(("col", "depth"), "row"),
            P("col"),
        ),
        check_vma=False,
    )
```
